32 devices in a mesh: band: 8 (over z, x), fld: 4 (over y, core).
Axes of the slice: x: 2, y: 2, z: 4, core: 2. Of those that a mesh axis runs over, the one named last changes fastest.
Arguments:
- grid_fields: bfloat16 [8, 2, 768, 3072], P('fld', None, 'band'), may hold values from -6 to 6
- legendre: bfloat16 [512, 2, 768, 513], P(('band', 'fld')), may hold values from -0.21875 to 0.21875
- slot_wave: int32 [1024], P(('band', 'fld')), may hold values from 0 to 1023, as said below
Outputs:
- spectrum: bfloat16 [512, 2, 8, 2, 513], P(('band', 'fld'))
The draws below stay inside these ranges and needn't reach their ends.
Inputs may be any that keep to these rules, and one draw needn't show every extreme that they name: `slot_wave`: for every q, slots 2 q and 2 q + 1 hold m and 1023 - m for some m below 512, or both hold 1024; every wavenumber below 1024 is held by exactly one slot.
All inputs are finite; a program needn't handle non-finite values.
Results may differ from the reference program's by a relative error of at most 0.0059.
Values may be sent and summed in bfloat16 or wider, within the bound.
No kernel may reach another device: no remote copies, remote signals or barrier semaphores. Data moves between devices by JAX's collectives and lax.ppermute only.
A program may use at most 64 MiB of HBM per device.

```python
import math
import jax
import jax.numpy as jnp
from jax import lax

NLON = 3072
HALF = 768
MM = 1024
FL = 8
SLOTS = 1024
PAIRS = 512
HCOL = 513


def draw_slot_wave(key, part):
    pair_slots = SLOTS // 2
    slot_order = jax.random.permutation(jax.random.fold_in(key, 11), pair_slots).astype(jnp.int32)
    half_count = MM // 2
    first_wave = jnp.where(slot_order < half_count, slot_order, MM)
    second_wave = jnp.where(slot_order < half_count, MM - 1 - slot_order, MM)
    return jnp.stack([first_wave, second_wave], axis=1).reshape(SLOTS).astype(jnp.int32)


def steps_of(key, dims, shards, low, high):
    def one(axis_at, blocks):
        heights = jax.random.uniform(jax.random.fold_in(jax.random.fold_in(key, 6), axis_at), (blocks,), jnp.float32, low / len(shards), high / len(shards))
        return jnp.repeat(jnp.exp(heights), dims[axis_at] // blocks).reshape((-1,) + (1,) * (len(dims) - axis_at - 1))

    level = one(*shards[0])
    for cut in shards[1:]:
        level = level * one(*cut)
    return level


def centred(rng, dims, deviation, bound, cuts=(), kind=jnp.bfloat16):
    array = deviation * jax.random.normal(rng, dims, jnp.float32)
    if cuts:
        array = array * steps_of(rng, dims, cuts, -0.22, 0.18)
    return jnp.clip(array, -bound, bound).astype(kind)


def setup_inputs(seed: int = 0) -> dict:
    splits = jax.random.split(jax.random.key(seed), 4)
    return {
        "grid_fields": centred(splits[0], (FL, 2, HALF, NLON), 1.0, 6.0, ((0, 4), (2, 8))),
        "legendre": centred(splits[1], (PAIRS, 2, HALF, HCOL), HALF ** -0.5, 0.21875, ((0, 32),)),
        "slot_wave": draw_slot_wave(jax.random.fold_in(splits[3], 71), 0),
    }


def build_table(wave_list, lon_count):
    lon_index = lax.broadcasted_iota(jnp.int32, (lon_count, wave_list.shape[0]), 0)
    phase_index = lon_index * wave_list[None, :] % lon_count
    phase_angle = phase_index.astype(jnp.float32) * (2.0 * math.pi / lon_count)
    norm_scale = 1.0 / math.sqrt(lon_count)
    live_mask = (wave_list < MM)[None, :]
    cosine = jnp.where(live_mask, jnp.cos(phase_angle) * norm_scale, 0.0)
    sine_part = jnp.where(live_mask, -jnp.sin(phase_angle) * norm_scale, 0.0)
    return jnp.stack([cosine, sine_part], axis=1).astype(jnp.bfloat16)

def reference(grid_fields, legendre, slot_wave):
    fields, hemispheres, half_rows, lon_count = grid_fields.shape
    fourier_table = build_table(jnp.arange(MM, dtype=jnp.int32), lon_count)
    grid_rows = grid_fields.reshape(fields * hemispheres * half_rows, lon_count).astype(jnp.float32)
    flat_table = fourier_table.reshape(lon_count, 2 * MM).astype(jnp.float32)
    fourier = jnp.dot(grid_rows, flat_table, precision=lax.Precision.HIGHEST)
    fourier = fourier.reshape(fields, hemispheres, half_rows, 2, MM)
    north_part = fourier[:, 0]
    south_part = fourier[:, 1]
    folded = jnp.stack([north_part + south_part, north_part - south_part], axis=1).astype(jnp.bfloat16)
    folded = jnp.concatenate([folded, jnp.zeros((fields, 2, half_rows, 2, 1), jnp.bfloat16)], axis=4)
    column = lax.broadcasted_iota(jnp.int32, (2, legendre.shape[3]), 1)
    parity = lax.broadcasted_iota(jnp.int32, (2, legendre.shape[3]), 0)

    def one_pair(pair_args):
        pair_wave, pair_table = pair_args
        columns = jnp.take(folded, pair_wave.astype(jnp.int32), axis=4).astype(jnp.float32)
        products = jnp.einsum('fphrk,phc->pfrkc', columns, pair_table.astype(jnp.float32), precision=lax.Precision.HIGHEST)
        first_count = (MM - pair_wave[0] + 1 - parity) // 2
        second_count = (pair_wave[0] + 2 - parity) // 2
        first_mask = (column < first_count)[:, None, None, :]
        second_mask = ((column >= first_count) & (column < first_count + second_count))[:, None, None, :]
        picked = jnp.where(first_mask, products[:, :, :, 0], jnp.where(second_mask, products[:, :, :, 1], 0.0))
        return picked.astype(jnp.bfloat16)
    return lax.map(one_pair, (slot_wave.reshape(-1, 2), legendre))
```

```python
import math

import jax
import jax.numpy as jnp
import numpy as np
from jax import lax
from jax.sharding import PartitionSpec as P

MM = 1024
AXES = ("band", "fld")


def half_table(lon_count):
    index = np.arange(MM // 2)
    even = np.where(index % 2 == 0, index, MM - 1 - index)
    waves = np.stack([even, MM - 1 - even])
    phase = waves[:, :, None] * np.arange(lon_count // 2)[None, None, :] % lon_count
    angle = phase.astype(np.float32) * np.float32(2.0 * math.pi / lon_count)
    scale = 1.0 / math.sqrt(lon_count)
    angle = angle.astype(np.float64)
    table = np.stack([np.cos(angle) * scale, -np.sin(angle) * scale], axis=1)
    return table.astype(np.float32).astype(jnp.bfloat16)


def local(grid_fields, legendre, slot_wave, *, devices):
    fields, _, lat_rows, lon_count = grid_fields.shape
    own_pairs = legendre.shape[0]
    own_waves = slot_wave.reshape(own_pairs, 2)[:, 0]
    wave_list = lax.all_to_all(
        jnp.broadcast_to(own_waves[None], (devices, own_pairs)), AXES, 0, 0, tiled=True
    )
    west = grid_fields[..., : lon_count // 2].astype(jnp.float32)
    east = grid_fields[..., lon_count // 2 :].astype(jnp.float32)
    halves = jnp.stack([west + east, west - east])
    north = halves[:, :, 0]
    south = halves[:, :, 1]
    folded = jnp.stack([north + south, north - south], axis=2).astype(jnp.bfloat16)
    folded = folded.reshape(2, fields * 2 * lat_rows, lon_count // 2)
    table = jnp.asarray(half_table(lon_count))
    fourier = jnp.einsum(
        "eril,eal->iera", table, folded, preferred_element_type=jnp.float32
    ).astype(jnp.bfloat16)
    order = (
        wave_list.reshape(-1)[:, None] == lax.broadcasted_iota(jnp.int32, (1, MM // 2), 1)
    ).astype(jnp.bfloat16)
    sent = jnp.einsum(
        "qi,ix->qx", order, fourier.reshape(MM // 2, -1), preferred_element_type=jnp.float32
    ).astype(jnp.bfloat16)
    got = lax.all_to_all(sent.reshape(devices, own_pairs, -1), AXES, 0, 0, tiled=True)
    bands = legendre.shape[2] // lat_rows
    got = got.reshape(bands, devices // bands, own_pairs, 2, 2, fields, 2, lat_rows)
    data = got.transpose(2, 6, 1, 5, 4, 3, 0, 7).reshape(own_pairs, 2, -1, bands * lat_rows)
    products = jnp.einsum("qpxj,qpjc->qpxc", data, legendre, preferred_element_type=jnp.float32)
    products = products.reshape(own_pairs, 2, -1, 2, 2, legendre.shape[3])
    first_wave = own_waves[:, None, None]
    parity = lax.broadcasted_iota(jnp.int32, (1, 2, 1), 1)
    column = lax.broadcasted_iota(jnp.int32, (1, 1, legendre.shape[3]), 2)
    first_count = (MM - first_wave + 1 - parity) // 2
    second_count = (first_wave + 2 - parity) // 2
    in_first = column < first_count
    live = (column < first_count + second_count) & (first_wave < MM)
    use_even = in_first == (first_wave % 2 == 0)
    spectrum = jnp.where(
        live[:, :, None, None],
        jnp.where(use_even[:, :, None, None], products[..., 0, :], products[..., 1, :]),
        0.0,
    )
    return spectrum.astype(jnp.bfloat16)


def solution(mesh):
    def run(grid_fields, legendre, slot_wave):
        return local(grid_fields, legendre, slot_wave, devices=mesh.size)

    return jax.shard_map(
        run,
        mesh=mesh,
        in_specs=(P("fld", None, "band", None), P(AXES, None, None, None), P(AXES)),
        out_specs=P(AXES, None, None, None, None),
        check_vma=False,
    )
```

```python
import functools
import math

import jax
import jax.numpy as jnp
import numpy as np
from jax import lax
from jax.experimental import pallas as pl
from jax.experimental.pallas import tpu as pltpu
from jax.sharding import PartitionSpec as P

MM = 1024
AXES = ("band", "fld")


def half_table(lon_count):
    index = np.arange(MM // 2)
    even = np.where(index % 2 == 0, index, MM - 1 - index)
    waves = np.stack([even, MM - 1 - even])
    phase = waves[:, :, None] * np.arange(lon_count // 2)[None, None, :] % lon_count
    angle = phase.astype(np.float32) * np.float32(2.0 * math.pi / lon_count)
    scale = 1.0 / math.sqrt(lon_count)
    angle = angle.astype(np.float64)
    table = np.stack([np.cos(angle) * scale, -np.sin(angle) * scale], axis=1)
    return table.astype(np.float32).astype(jnp.bfloat16)


def general(grid_fields, legendre, slot_wave, *, devices):
    fields, _, lat_rows, lon_count = grid_fields.shape
    own_pairs = legendre.shape[0]
    own_waves = slot_wave.reshape(own_pairs, 2)[:, 0]
    wave_list = lax.all_to_all(
        jnp.broadcast_to(own_waves[None], (devices, own_pairs)), AXES, 0, 0, tiled=True
    )
    west = grid_fields[..., : lon_count // 2].astype(jnp.float32)
    east = grid_fields[..., lon_count // 2 :].astype(jnp.float32)
    halves = jnp.stack([west + east, west - east])
    north = halves[:, :, 0]
    south = halves[:, :, 1]
    folded = jnp.stack([north + south, north - south], axis=2).astype(jnp.bfloat16)
    folded = folded.reshape(2, fields * 2 * lat_rows, lon_count // 2)
    table = jnp.asarray(half_table(lon_count))
    fourier = jnp.einsum(
        "eril,eal->iera", table, folded, preferred_element_type=jnp.float32
    ).astype(jnp.bfloat16)
    order = (
        wave_list.reshape(-1)[:, None] == lax.broadcasted_iota(jnp.int32, (1, MM // 2), 1)
    ).astype(jnp.bfloat16)
    sent = jnp.einsum(
        "qi,ix->qx", order, fourier.reshape(MM // 2, -1), preferred_element_type=jnp.float32
    ).astype(jnp.bfloat16)
    got = lax.all_to_all(sent.reshape(devices, own_pairs, -1), AXES, 0, 0, tiled=True)
    bands = legendre.shape[2] // lat_rows
    got = got.reshape(bands, devices // bands, own_pairs, 2, 2, fields, 2, lat_rows)
    data = got.transpose(2, 6, 1, 5, 4, 3, 0, 7).reshape(own_pairs, 2, -1, bands * lat_rows)
    products = jnp.einsum("qpxj,qpjc->qpxc", data, legendre, preferred_element_type=jnp.float32)
    products = products.reshape(own_pairs, 2, -1, 2, 2, legendre.shape[3])
    first_wave = own_waves[:, None, None]
    parity = lax.broadcasted_iota(jnp.int32, (1, 2, 1), 1)
    column = lax.broadcasted_iota(jnp.int32, (1, 1, legendre.shape[3]), 2)
    first_count = (MM - first_wave + 1 - parity) // 2
    second_count = (first_wave + 2 - parity) // 2
    in_first = column < first_count
    live = (column < first_count + second_count) & (first_wave < MM)
    use_even = in_first == (first_wave % 2 == 0)
    spectrum = jnp.where(
        live[:, :, None, None],
        jnp.where(use_even[:, :, None, None], products[..., 0, :], products[..., 1, :]),
        0.0,
    )
    return spectrum.astype(jnp.bfloat16)


NT = (((1,), (1,)), ((), ()))
GROUP = 4
AHEAD = 4


def repeat_kernel(wave, out):
    out[...] = jnp.broadcast_to(wave[...], out.shape)


def repeated(slot_wave, count):
    whole = pl.BlockSpec(memory_space=pltpu.VMEM)
    return pl.pallas_call(
        repeat_kernel,
        in_specs=[whole],
        out_specs=whole,
        out_shape=jax.ShapeDtypeStruct((count, 1, slot_wave.shape[0]), jnp.int32),
        name="repeated",
    )(slot_wave.reshape(1, 1, -1))


def transform_kernel(me, grid, table, out, folded):
    fields, _, rows, lons = grid.shape
    half = lons // 2
    turn = (me[0] >> 2) & 3
    kind = pl.program_id(0)

    for field in range(fields):
        for row in range(0, rows, 16):
            part = pl.ds(row, 16)
            west = [grid[field, side, part, :half].astype(jnp.float32) for side in range(2)]
            east = [grid[field, side, part, half:].astype(jnp.float32) for side in range(2)]
            north, south = [
                jnp.where(kind == 0, west[side] + east[side], west[side] - east[side])
                for side in range(2)
            ]
            for parity in range(2):
                value = north + south if parity == 0 else north - south
                place = (field * 2 + parity + turn) & 3
                at = pl.multiple_of(place * rows + row, 16)
                folded[pl.ds(at, 16), :] = value.astype(jnp.bfloat16)

    for part in range(2):
        out[part] = lax.dot_general(
            table[part], folded[...], NT, preferred_element_type=jnp.float32
        ).astype(jnp.bfloat16)


def transform(me, grid_fields, table):
    fields, _, rows, lons = grid_fields.shape
    kinds, waves, half = table.shape
    lanes = fields * 2 * rows
    return pl.pallas_call(
        transform_kernel,
        grid_spec=pltpu.PrefetchScalarGridSpec(
            num_scalar_prefetch=1,
            grid=(2,),
            in_specs=[
                pl.BlockSpec(grid_fields.shape, lambda k, me: (0, 0, 0, 0)),
                pl.BlockSpec((2, waves, half), lambda k, me: (k, 0, 0)),
            ],
            out_specs=pl.BlockSpec((2, waves, lanes), lambda k, me: (k, 0, 0)),
            scratch_shapes=[pltpu.VMEM((lanes, half), jnp.bfloat16)],
        ),
        out_shape=jax.ShapeDtypeStruct((kinds, waves, lanes), jnp.bfloat16),
        compiler_params=pltpu.CompilerParams(vmem_limit_bytes=24 << 20),
        cost_estimate=pl.CostEstimate(
            flops=2 * kinds * waves * half * lanes, bytes_accessed=10 << 20, transcendentals=0
        ),
        name="transform",
    )(me, grid_fields, table)


def order_kernel(waves, fourier, out, square, picks, rows_f32):
    kinds, count, lanes = fourier.shape
    devices, size, _ = out.shape
    pairs = size // kinds
    slots = devices * pairs
    square[...] = jnp.zeros_like(square)
    for device in range(devices):
        square[device : device + 1, : 2 * pairs] = waves[device]
    square[...] = square[...].T
    number = lax.broadcasted_iota(jnp.int32, (pairs, count), 1)
    firsts = square[pl.ds(0, pairs, stride=2), :]
    for device in range(devices):
        wave = firsts[:, device : device + 1]
        picks[device * pairs : (device + 1) * pairs, :] = (
            jnp.where(wave == number, 1.0, 0.0).astype(jnp.bfloat16)
        )
    for kind in range(kinds):
        got = jnp.dot(picks[...], fourier[kind], preferred_element_type=jnp.float32)
        for tile in range(lanes // 128):
            rows_f32[tile, pl.ds(kind, slots, stride=kinds), :] = got[:, tile * 128 : tile * 128 + 128]
    for device in range(devices):
        for tile in range(lanes // 128):
            out[device, :, tile * 128 : tile * 128 + 128] = rows_f32[
                tile, device * size : (device + 1) * size, :
            ].astype(jnp.bfloat16)


def ordered(waves, fourier, pairs):
    kinds, count, lanes = fourier.shape
    devices = waves.shape[0]
    slots = devices * pairs
    whole = pl.BlockSpec(memory_space=pltpu.VMEM)
    return pl.pallas_call(
        order_kernel,
        in_specs=[whole, whole],
        out_specs=whole,
        scratch_shapes=[
            pltpu.VMEM((128, 128), jnp.int32),
            pltpu.VMEM((slots, count), jnp.bfloat16),
            pltpu.VMEM((lanes // 128, kinds * slots, 128), jnp.float32),
        ],
        out_shape=jax.ShapeDtypeStruct((devices, kinds * pairs, lanes), jnp.bfloat16),
        compiler_params=pltpu.CompilerParams(vmem_limit_bytes=24 << 20),
        cost_estimate=pl.CostEstimate(
            flops=2 * slots * kinds * count * lanes, bytes_accessed=4 << 20, transcendentals=0
        ),
        name="ordered",
    )(waves, fourier)


def turned_kernel(table, out, last):
    columns, _, lat = table.shape[1:]
    main = columns - 1
    out[0] = table[0, :main].reshape(2 * main, lat).T
    last[0] = table[0, main]


def turned(table):
    pairs, columns, _, lat = table.shape
    wide = 2 * columns - 2
    return pl.pallas_call(
        turned_kernel,
        grid=(pairs,),
        in_specs=[pl.BlockSpec((1, columns, 2, lat), lambda i: (i, 0, 0, 0))],
        out_specs=[
            pl.BlockSpec((1, lat, wide), lambda i: (i, 0, 0)),
            pl.BlockSpec((1, 2, lat), lambda i: (i, 0, 0)),
        ],
        out_shape=[
            jax.ShapeDtypeStruct((pairs, lat, wide), jnp.bfloat16),
            jax.ShapeDtypeStruct((pairs, 2, lat), jnp.bfloat16),
        ],
        compiler_params=pltpu.CompilerParams(vmem_limit_bytes=16 << 20),
        cost_estimate=pl.CostEstimate(
            flops=20 << 30, bytes_accessed=60 << 20, transcendentals=0
        ),
        name="turned",
    )(table)


def legendre_kernel(waves, blocks, table, last, spread, out, held, data, lines, sems):
    pairs, lat, wide = table.shape
    lanes = blocks.shape[2]
    rows = lanes // 4
    columns = wide // 2 + 1
    copies = [
        pltpu.make_async_copy(table.at[pair], held.at[pair], sems.at[pair]) for pair in range(pairs)
    ]
    for pair in range(AHEAD):
        copies[pair].start()
    lane = lax.broadcasted_iota(jnp.int32, (4 * GROUP, lanes), 1)
    for group in range(pairs // GROUP):
        for half in range(2):
            for field in range(4):
                have = [
                    blocks[
                        (half * 4 + band) * 4 + field, group * 4 * GROUP : (group + 1) * 4 * GROUP, :
                    ].astype(jnp.float32)
                    for band in range(4)
                ]
                for turn in range(4):
                    value = have[-turn % 4]
                    for place in range(1, 4):
                        value = jnp.where(lane >= place * rows, have[(place - turn) % 4], value)
                    if turn:
                        value = pltpu.roll(value, lanes - turn * rows, 1)
                    line = (field * 2 + turn // 2) * 2
                    for pair in range(GROUP):
                        for kind in range(2):
                            data[
                                group * GROUP + pair,
                                turn % 2,
                                pl.ds(kind * 16 + line, 2),
                                half * lanes : (half + 1) * lanes,
                            ] = value[pair * 4 + kind * 2 : pair * 4 + kind * 2 + 2]

    index = lax.broadcasted_iota(jnp.int32, (32, wide), 1)
    even = index & 1 == 0
    index = index[:16]
    parity, column = index & 1, index >> 1
    for group in range(pairs // GROUP):
        for pair in range(group * GROUP, (group + 1) * GROUP):
            copies[pair].wait()
            if pair + AHEAD < pairs:
                copies[pair + AHEAD].start()
            here = data[pair].reshape(64, lat).astype(jnp.bfloat16)
            both = jnp.dot(here, held[pair], preferred_element_type=jnp.float32)
            value = jnp.where(even, both[:32], both[32:])
            wave = waves[pair]
            first_count = (MM - wave + 1 - parity) >> 1
            second_count = (wave + 2 - parity) >> 1
            live = (column < first_count + second_count) & (wave < MM)
            in_first = jnp.where(column < first_count, 1, 0)
            value = jnp.where(in_first != (wave & 1), value[:16], value[16:])
            lines[pair * 16 : pair * 16 + 16, :] = jnp.where(live, value, 0.0).astype(jnp.bfloat16)

        top = group * GROUP * 16
        for block in range(wide // 256):
            apart = jnp.dot(
                lines[top : top + GROUP * 16, block * 256 : block * 256 + 256],
                spread[...],
                preferred_element_type=jnp.float32,
            ).astype(jnp.bfloat16)
            for pair in range(GROUP):
                for side in range(2):
                    piece = apart[pair * 16 : pair * 16 + 16, side * 128 : side * 128 + 128]
                    out[group * GROUP + pair, side, :, :, block * 128 : block * 128 + 128] = (
                        piece.reshape(8, 2, 128)
                    )
    for pair in range(pairs):
        wave = waves[pair]
        for side in range(2):
            value = jnp.sum(
                data[pair, side] * last[pair, side : side + 1].astype(jnp.float32), axis=1, keepdims=True
            )
            first_count = (MM - wave + 1 - side) >> 1
            second_count = (wave + 2 - side) >> 1
            live = (columns - 1 < first_count + second_count) & (wave < MM)
            in_first = jnp.where(columns - 1 < first_count, 1, 0)
            value = jnp.where(in_first != (wave & 1), value[:16], value[16:])
            value = jnp.where(live, value, 0.0).astype(jnp.bfloat16)
            out[pair, side, :, :, columns - 1 :] = value.reshape(8, 2, 1)


def legendre_product(waves, blocks, table, last):
    pairs, lat, wide = table.shape
    columns = wide // 2 + 1
    lane = np.arange(256)
    spread = np.zeros((256, 256), np.float32)
    spread[lane, (lane % 2) * 128 + lane // 2] = 1.0
    whole = pl.BlockSpec(memory_space=pltpu.VMEM)
    return pl.pallas_call(
        legendre_kernel,
        in_specs=[
            pl.BlockSpec(memory_space=pltpu.SMEM),
            whole,
            pl.BlockSpec(memory_space=pl.ANY),
            whole,
            whole,
        ],
        out_specs=whole,
        scratch_shapes=[
            pltpu.VMEM((pairs, lat, wide), jnp.bfloat16),
            pltpu.VMEM((pairs, 2, 32, lat), jnp.float32),
            pltpu.VMEM((16 * pairs, wide), jnp.bfloat16),
            pltpu.SemaphoreType.DMA((pairs,)),
        ],
        out_shape=jax.ShapeDtypeStruct((pairs, 2, 8, 2, columns), jnp.bfloat16),
        compiler_params=pltpu.CompilerParams(vmem_limit_bytes=48 << 20),
        cost_estimate=pl.CostEstimate(flops=8 << 30, bytes_accessed=30 << 20, transcendentals=0),
        name="legendre_product",
    )(waves, blocks, table, last, jnp.asarray(spread.astype(jnp.bfloat16)))


def local(grid_fields, legendre, slot_wave, *, devices):
    lon_count = grid_fields.shape[3]
    own_pairs = legendre.shape[0]
    me = lax.axis_index(AXES).astype(jnp.int32).reshape(1)
    own_waves = slot_wave.reshape(own_pairs, 2)[:, 0]
    waves = lax.all_to_all(repeated(slot_wave, devices), AXES, 0, 0, tiled=True)
    table = jnp.asarray(half_table(lon_count).reshape(4, MM // 2, lon_count // 2))
    fourier = transform(me, HBM(grid_fields), HBM(table))
    sent = ordered(waves, fourier, own_pairs)
    got = lax.all_to_all(sent, AXES, 0, 0, tiled=True)
    rows, last = turned(HBM(legendre.transpose(0, 3, 1, 2)))
    return legendre_product(own_waves, got, HBM(rows), last)


def HBM(array):
    return pltpu.with_memory_space_constraint(array, pltpu.HBM)


def fits(mesh, grid_fields, legendre):
    fields, _, rows, _ = grid_fields.shape
    return (
        mesh.shape["band"] == 8
        and mesh.shape["fld"] == 4
        and fields == 8
        and rows % 128 == 0
        and rows * 4 // 8 % 128 == 0
        and legendre.shape[3] % 128 == 1
        and legendre.shape[0] == MM // 2
    )


def solution(mesh):
    def run(grid_fields, legendre, slot_wave):
        part = local if fits(mesh, grid_fields, legendre) else general
        return jax.shard_map(
            functools.partial(part, devices=mesh.size),
            mesh=mesh,
            in_specs=(P("fld", None, "band", None), P(AXES, None, None, None), P(AXES)),
            out_specs=P(AXES, None, None, None, None),
            check_vma=False,
        )(grid_fields, legendre, slot_wave)

    return run
```

```python
import functools
import math

import jax
import jax.numpy as jnp
import numpy as np
from jax import lax
from jax.experimental import pallas as pl
from jax.experimental.pallas import tpu as pltpu
from jax.sharding import PartitionSpec as P

MM = 1024
AXES = ("band", "fld")


def half_table(lon_count, index):
    even = np.where(index % 2 == 0, index, MM - 1 - index)
    waves = np.stack([even, MM - 1 - even])
    phase = waves[:, :, None] * np.arange(lon_count // 2)[None, None, :] % lon_count
    angle = phase.astype(np.float32) * np.float32(2.0 * math.pi / lon_count)
    scale = 1.0 / math.sqrt(lon_count)
    angle = angle.astype(np.float64)
    table = np.stack([np.cos(angle) * scale, -np.sin(angle) * scale], axis=1)
    return table.astype(np.float32).astype(jnp.bfloat16)


def general(grid_fields, legendre, slot_wave, *, devices):
    fields, _, lat_rows, lon_count = grid_fields.shape
    own_pairs = legendre.shape[0]
    own_waves = slot_wave.reshape(own_pairs, 2)[:, 0]
    wave_list = lax.all_to_all(
        jnp.broadcast_to(own_waves[None], (devices, own_pairs)), AXES, 0, 0, tiled=True
    )
    west = grid_fields[..., : lon_count // 2].astype(jnp.float32)
    east = grid_fields[..., lon_count // 2 :].astype(jnp.float32)
    halves = jnp.stack([west + east, west - east])
    north = halves[:, :, 0]
    south = halves[:, :, 1]
    folded = jnp.stack([north + south, north - south], axis=2).astype(jnp.bfloat16)
    folded = folded.reshape(2, fields * 2 * lat_rows, lon_count // 2)
    table = jnp.asarray(half_table(lon_count, np.arange(MM // 2)))
    fourier = jnp.einsum(
        "eril,eal->iera", table, folded, preferred_element_type=jnp.float32
    ).astype(jnp.bfloat16)
    order = (
        wave_list.reshape(-1)[:, None] == lax.broadcasted_iota(jnp.int32, (1, MM // 2), 1)
    ).astype(jnp.bfloat16)
    sent = jnp.einsum(
        "qi,ix->qx", order, fourier.reshape(MM // 2, -1), preferred_element_type=jnp.float32
    ).astype(jnp.bfloat16)
    got = lax.all_to_all(sent.reshape(devices, own_pairs, -1), AXES, 0, 0, tiled=True)
    bands = legendre.shape[2] // lat_rows
    got = got.reshape(bands, devices // bands, own_pairs, 2, 2, fields, 2, lat_rows)
    data = got.transpose(2, 6, 1, 5, 4, 3, 0, 7).reshape(own_pairs, 2, -1, bands * lat_rows)
    products = jnp.einsum("qpxj,qpjc->qpxc", data, legendre, preferred_element_type=jnp.float32)
    products = products.reshape(own_pairs, 2, -1, 2, 2, legendre.shape[3])
    first_wave = own_waves[:, None, None]
    parity = lax.broadcasted_iota(jnp.int32, (1, 2, 1), 1)
    column = lax.broadcasted_iota(jnp.int32, (1, 1, legendre.shape[3]), 2)
    first_count = (MM - first_wave + 1 - parity) // 2
    second_count = (first_wave + 2 - parity) // 2
    in_first = column < first_count
    live = (column < first_count + second_count) & (first_wave < MM)
    use_even = in_first == (first_wave % 2 == 0)
    spectrum = jnp.where(
        live[:, :, None, None],
        jnp.where(use_even[:, :, None, None], products[..., 0, :], products[..., 1, :]),
        0.0,
    )
    return spectrum.astype(jnp.bfloat16)


NT = (((1,), (1,)), ((), ()))
GROUP = 4
AHEAD = 16


def repeat_kernel(wave, out):
    out[...] = jnp.broadcast_to(wave[...], out.shape)


def repeated(slot_wave, count):
    whole = pl.BlockSpec(memory_space=pltpu.VMEM)
    return pl.pallas_call(
        repeat_kernel,
        in_specs=[whole],
        out_specs=whole,
        out_shape=jax.ShapeDtypeStruct((count, 1, slot_wave.shape[0]), jnp.int32),
        name="repeated",
    )(slot_wave.reshape(1, 1, -1))


def quarter_order(row):
    low = 4 * ((row % (MM // 4)) // 2)
    return low + (row // (MM // 4)) + (row % 2) * (3 - 2 * (row // (MM // 4)))


def transform_kernel(me, grid, table, out, grid_here, table_here, folded, grid_sems, table_sems):
    fields, _, rows, lons = grid_here.shape
    half = lons // 2
    quarter = half // 2
    turn = (me[0] >> 2) & 3
    grid_copies = [
        pltpu.make_async_copy(grid.at[field], grid_here.at[field], grid_sems.at[field])
        for field in range(fields)
    ]
    table_copies = [
        pltpu.make_async_copy(table.at[part], table_here.at[part], table_sems.at[part])
        for part in range(table.shape[0])
    ]
    for copy in grid_copies + table_copies:
        copy.start()

    def fold(kind, field):
        for row in range(0, rows, 16):
            part = pl.ds(row, 16)
            west = [grid_here[field, side, part, :half].astype(jnp.float32) for side in range(2)]
            east = [grid_here[field, side, part, half:].astype(jnp.float32) for side in range(2)]
            north, south = [
                west[side] + east[side] if kind == 0 else west[side] - east[side]
                for side in range(2)
            ]
            for parity in range(2):
                value = north + south if parity == 0 else north - south
                if kind == 0:
                    left, right = value[:, :quarter], value[:, quarter:]
                    value = jnp.concatenate([left + right, left - right], axis=1)
                place = (field * 2 + parity + turn) & 3
                at = pl.multiple_of(place * rows + row, 16)
                folded[kind, pl.ds(at, 16), :] = value.astype(jnp.bfloat16)

    def product(first, second):
        return lax.dot_general(first, second, NT, preferred_element_type=jnp.float32).astype(
            jnp.bfloat16
        )

    for field in range(fields):
        grid_copies[field].wait()
        fold(0, field)
    table_copies[0].wait()
    waves = table.shape[1]
    half_rows = waves // 2
    for which in range(2):
        lanes = slice(which * quarter, (which + 1) * quarter)
        got = product(table_here[0, :, lanes], folded[0, :, lanes])
        for part in range(2):
            out[part, which * half_rows : (which + 1) * half_rows] = got[
                part * half_rows : (part + 1) * half_rows
            ]
    for field in range(fields):
        fold(1, field)
    for part in range(2):
        table_copies[1 + part].wait()
    got = product(table_here[1:].reshape(2 * waves, half), folded[1])
    for part in range(2):
        out[2 + part] = got[part * waves : (part + 1) * waves]


def transform(me, grid_fields, table):
    fields, _, rows, lons = grid_fields.shape
    parts, waves, half = table.shape
    lanes = fields * 2 * rows
    return pl.pallas_call(
        transform_kernel,
        in_specs=[
            pl.BlockSpec(memory_space=pltpu.SMEM),
            pl.BlockSpec(memory_space=pl.ANY),
            pl.BlockSpec(memory_space=pl.ANY),
        ],
        out_specs=pl.BlockSpec(memory_space=pltpu.VMEM),
        scratch_shapes=[
            pltpu.VMEM(grid_fields.shape, jnp.bfloat16),
            pltpu.VMEM(table.shape, jnp.bfloat16),
            pltpu.VMEM((2, lanes, half), jnp.bfloat16),
            pltpu.SemaphoreType.DMA((fields,)),
            pltpu.SemaphoreType.DMA((parts,)),
        ],
        out_shape=jax.ShapeDtypeStruct((4, waves, lanes), jnp.bfloat16),
        compiler_params=pltpu.CompilerParams(vmem_limit_bytes=24 << 20),
        cost_estimate=pl.CostEstimate(
            flops=6 * waves * half * lanes, bytes_accessed=10 << 20, transcendentals=0
        ),
        name="transform",
    )(me, grid_fields, table)


def transform_table(lon_count):
    full = half_table(lon_count, quarter_order(np.arange(MM // 2)))
    short = full[0, :, :, : lon_count // 4].reshape(2, 2, MM // 4, lon_count // 4)
    short = short.transpose(0, 2, 1, 3).reshape(MM // 2, lon_count // 2)
    return np.stack([short, full[1, 0], full[1, 1]])


def order_kernel(waves, fourier, out, square, picks, rows_f32, staged, sems):
    kinds, count, lanes = fourier.shape
    devices, size, _ = out.shape
    pairs = size // kinds
    slots = devices * pairs
    square[...] = jnp.zeros_like(square)
    for device in range(devices):
        square[device : device + 1, : 2 * pairs] = waves[device]
    square[...] = square[...].T
    number = quarter_order(lax.broadcasted_iota(jnp.int32, (pairs, count), 1))
    firsts = square[pl.ds(0, pairs, stride=2), :]
    for device in range(devices):
        wave = firsts[:, device : device + 1]
        picks[device * pairs : (device + 1) * pairs, :] = (
            jnp.where(wave == number, 1.0, 0.0).astype(jnp.bfloat16)
        )
    for kind in range(kinds):
        got = jnp.dot(picks[...], fourier[kind], preferred_element_type=jnp.float32)
        for tile in range(lanes // 128):
            rows_f32[tile, pl.ds(kind, slots, stride=kinds), :] = got[:, tile * 128 : tile * 128 + 128]
    copies = []
    for device in range(devices):
        for tile in range(lanes // 128):
            staged[device, :, tile * 128 : tile * 128 + 128] = rows_f32[
                tile, device * size : (device + 1) * size, :
            ].astype(jnp.bfloat16)
        if device % 8 == 7:
            part = pl.ds(device - 7, 8)
            copy = pltpu.make_async_copy(staged.at[part], out.at[part], sems.at[device // 8])
            copy.start()
            copies.append(copy)
    for copy in copies:
        copy.wait()


def ordered(waves, fourier, pairs):
    kinds, count, lanes = fourier.shape
    devices = waves.shape[0]
    slots = devices * pairs
    whole = pl.BlockSpec(memory_space=pltpu.VMEM)
    return pl.pallas_call(
        order_kernel,
        in_specs=[whole, whole],
        out_specs=pl.BlockSpec(memory_space=pl.ANY),
        scratch_shapes=[
            pltpu.VMEM((128, 128), jnp.int32),
            pltpu.VMEM((slots, count), jnp.bfloat16),
            pltpu.VMEM((lanes // 128, kinds * slots, 128), jnp.float32),
            pltpu.VMEM((devices, kinds * pairs, lanes), jnp.bfloat16),
            pltpu.SemaphoreType.DMA((devices // 8,)),
        ],
        out_shape=jax.ShapeDtypeStruct((devices, kinds * pairs, lanes), jnp.bfloat16),
        compiler_params=pltpu.CompilerParams(vmem_limit_bytes=24 << 20),
        cost_estimate=pl.CostEstimate(
            flops=2 * slots * kinds * count * lanes, bytes_accessed=4 << 20, transcendentals=0
        ),
        name="ordered",
    )(waves, fourier)


def turned_kernel(table, out, last):
    columns, _, lat = table.shape[1:]
    main = columns - 1
    out[0] = table[0, :main].reshape(2 * main, lat).T
    last[0] = table[0, main]


def turned(table):
    pairs, columns, _, lat = table.shape
    wide = 2 * columns - 2
    return pl.pallas_call(
        turned_kernel,
        grid=(pairs,),
        in_specs=[pl.BlockSpec((1, columns, 2, lat), lambda i: (i, 0, 0, 0))],
        out_specs=[
            pl.BlockSpec((1, lat, wide), lambda i: (i, 0, 0)),
            pl.BlockSpec((1, 2, lat), lambda i: (i, 0, 0)),
        ],
        out_shape=[
            jax.ShapeDtypeStruct((pairs, lat, wide), jnp.bfloat16),
            jax.ShapeDtypeStruct((pairs, 2, lat), jnp.bfloat16),
        ],
        compiler_params=pltpu.CompilerParams(vmem_limit_bytes=16 << 20),
        cost_estimate=pl.CostEstimate(
            flops=20 << 30, bytes_accessed=60 << 20, transcendentals=0
        ),
        name="turned",
    )(table)


def legendre_kernel(waves, blocks, table, last, spread, out, held, data, lines, staged, sems, out_sems):
    pairs, lat, wide = table.shape
    lanes = blocks.shape[2]
    rows = lanes // 4
    columns = wide // 2 + 1
    copies = [
        pltpu.make_async_copy(table.at[pair], held.at[pair], sems.at[pair]) for pair in range(pairs)
    ]
    for pair in range(AHEAD):
        copies[pair].start()
    lane = lax.broadcasted_iota(jnp.int32, (4 * GROUP, lanes), 1)
    for group in range(pairs // GROUP):
        for half in range(2):
            for field in range(4):
                have = [
                    blocks[
                        (half * 4 + band) * 4 + field, group * 4 * GROUP : (group + 1) * 4 * GROUP, :
                    ].astype(jnp.float32)
                    for band in range(4)
                ]
                for turn in range(4):
                    value = have[-turn % 4]
                    for place in range(1, 4):
                        value = jnp.where(lane >= place * rows, have[(place - turn) % 4], value)
                    if turn:
                        value = pltpu.roll(value, lanes - turn * rows, 1)
                    line = (field * 2 + turn // 2) * 2
                    for pair in range(GROUP):
                        for kind in range(2):
                            data[
                                group * GROUP + pair,
                                turn % 2,
                                pl.ds(kind * 16 + line, 2),
                                half * lanes : (half + 1) * lanes,
                            ] = value[pair * 4 + kind * 2 : pair * 4 + kind * 2 + 2]

    for pair in range(pairs):
        wave = waves[pair]
        for side in range(2):
            value = jnp.sum(
                data[pair, side] * last[pair, side : side + 1].astype(jnp.float32), axis=1, keepdims=True
            )
            first_count = (MM - wave + 1 - side) >> 1
            second_count = (wave + 2 - side) >> 1
            live = (columns - 1 < first_count + second_count) & (wave < MM)
            in_first = jnp.where(columns - 1 < first_count, 1, 0)
            value = jnp.where(in_first != (wave & 1), value[:16], value[16:])
            value = jnp.where(live, value, 0.0).astype(jnp.bfloat16)
            staged[pair, side, :, :, columns - 1 :] = value.reshape(8, 2, 1)

    index = lax.broadcasted_iota(jnp.int32, (32, wide), 1)
    even = index & 1 == 0
    index = index[:16]
    parity, column = index & 1, index >> 1
    written = []
    groups = [GROUP] * (pairs // GROUP - 1) + [GROUP // 2, GROUP // 4, GROUP // 4]
    for group, count in enumerate(groups):
        start = sum(groups[:group])
        for pair in range(start, start + count):
            copies[pair].wait()
            if pair + AHEAD < pairs:
                copies[pair + AHEAD].start()
            here = data[pair].reshape(64, lat).astype(jnp.bfloat16)
            both = jnp.dot(here, held[pair], preferred_element_type=jnp.float32)
            value = jnp.where(even, both[:32], both[32:])
            wave = waves[pair]
            first_count = (MM - wave + 1 - parity) >> 1
            second_count = (wave + 2 - parity) >> 1
            live = (column < first_count + second_count) & (wave < MM)
            in_first = jnp.where(column < first_count, 1, 0)
            value = jnp.where(in_first != (wave & 1), value[:16], value[16:])
            lines[pair * 16 : pair * 16 + 16, :] = jnp.where(live, value, 0.0).astype(jnp.bfloat16)

        top = start * 16
        for block in range(wide // 256):
            apart = jnp.dot(
                lines[top : top + count * 16, block * 256 : block * 256 + 256],
                spread[...],
                preferred_element_type=jnp.float32,
            ).astype(jnp.bfloat16)
            for pair in range(count):
                for side in range(2):
                    piece = apart[pair * 16 : pair * 16 + 16, side * 128 : side * 128 + 128]
                    staged[start + pair, side, :, :, block * 128 : block * 128 + 128] = (
                        piece.reshape(8, 2, 128)
                    )
        part = pl.ds(start, count)
        written.append(pltpu.make_async_copy(staged.at[part], out.at[part], out_sems.at[group]))
        written[-1].start()
    for copy in written:
        copy.wait()


def legendre_product(waves, blocks, table, last):
    pairs, lat, wide = table.shape
    columns = wide // 2 + 1
    lane = np.arange(256)
    spread = np.zeros((256, 256), np.float32)
    spread[lane, (lane % 2) * 128 + lane // 2] = 1.0
    whole = pl.BlockSpec(memory_space=pltpu.VMEM)
    return pl.pallas_call(
        legendre_kernel,
        in_specs=[
            pl.BlockSpec(memory_space=pltpu.SMEM),
            whole,
            pl.BlockSpec(memory_space=pl.ANY),
            whole,
            whole,
        ],
        out_specs=pl.BlockSpec(memory_space=pl.ANY),
        scratch_shapes=[
            pltpu.VMEM((pairs, lat, wide), jnp.bfloat16),
            pltpu.VMEM((pairs, 2, 32, lat), jnp.float32),
            pltpu.VMEM((16 * pairs, wide), jnp.bfloat16),
            pltpu.VMEM((pairs, 2, 8, 2, columns), jnp.bfloat16),
            pltpu.SemaphoreType.DMA((pairs,)),
            pltpu.SemaphoreType.DMA((pairs // GROUP + 2,)),
        ],
        out_shape=jax.ShapeDtypeStruct((pairs, 2, 8, 2, columns), jnp.bfloat16),
        compiler_params=pltpu.CompilerParams(vmem_limit_bytes=48 << 20),
        cost_estimate=pl.CostEstimate(flops=8 << 30, bytes_accessed=30 << 20, transcendentals=0),
        name="legendre_product",
    )(waves, blocks, table, last, jnp.asarray(spread.astype(jnp.bfloat16)))


def local(grid_fields, legendre, slot_wave, *, devices):
    lon_count = grid_fields.shape[3]
    own_pairs = legendre.shape[0]
    me = lax.axis_index(AXES).astype(jnp.int32).reshape(1)
    own_waves = slot_wave.reshape(own_pairs, 2)[:, 0]
    waves = lax.all_to_all(repeated(slot_wave, devices), AXES, 0, 0, tiled=True)
    table = jnp.asarray(transform_table(lon_count))
    fourier = transform(me, HBM(grid_fields), HBM(table))
    sent = ordered(waves, fourier, own_pairs)
    got = lax.all_to_all(sent, AXES, 0, 0, tiled=True)
    rows, last = turned(HBM(legendre.transpose(0, 3, 1, 2)))
    return legendre_product(own_waves, got, HBM(rows), last)


def HBM(array):
    return pltpu.with_memory_space_constraint(array, pltpu.HBM)


def fits(mesh, grid_fields, legendre):
    fields, _, rows, _ = grid_fields.shape
    return (
        mesh.shape["band"] == 8
        and mesh.shape["fld"] == 4
        and fields == 8
        and rows % 128 == 0
        and rows * 4 // 8 % 128 == 0
        and legendre.shape[3] % 128 == 1
        and legendre.shape[0] == MM // 2
    )


def solution(mesh):
    def run(grid_fields, legendre, slot_wave):
        part = local if fits(mesh, grid_fields, legendre) else general
        return jax.shard_map(
            functools.partial(part, devices=mesh.size),
            mesh=mesh,
            in_specs=(P("fld", None, "band", None), P(AXES, None, None, None), P(AXES)),
            out_specs=P(AXES, None, None, None, None),
            check_vma=False,
        )(grid_fields, legendre, slot_wave)

    return run
```

```python
import functools
import math

import jax
import jax.numpy as jnp
import numpy as np
from jax import lax
from jax.experimental import pallas as pl
from jax.experimental.pallas import tpu as pltpu
from jax.sharding import PartitionSpec as P

MM = 1024
AXES = ("band", "fld")


def half_table(lon_count, index):
    even = np.where(index % 2 == 0, index, MM - 1 - index)
    waves = np.stack([even, MM - 1 - even])
    phase = waves[:, :, None] * np.arange(lon_count // 2)[None, None, :] % lon_count
    angle = phase.astype(np.float32) * np.float32(2.0 * math.pi / lon_count)
    scale = 1.0 / math.sqrt(lon_count)
    angle = angle.astype(np.float64)
    table = np.stack([np.cos(angle) * scale, -np.sin(angle) * scale], axis=1)
    return table.astype(np.float32).astype(jnp.bfloat16)


def general(grid_fields, legendre, slot_wave, *, devices):
    fields, _, lat_rows, lon_count = grid_fields.shape
    own_pairs = legendre.shape[0]
    own_waves = slot_wave.reshape(own_pairs, 2)[:, 0]
    wave_list = lax.all_to_all(
        jnp.broadcast_to(own_waves[None], (devices, own_pairs)), AXES, 0, 0, tiled=True
    )
    west = grid_fields[..., : lon_count // 2].astype(jnp.float32)
    east = grid_fields[..., lon_count // 2 :].astype(jnp.float32)
    halves = jnp.stack([west + east, west - east])
    north = halves[:, :, 0]
    south = halves[:, :, 1]
    folded = jnp.stack([north + south, north - south], axis=2).astype(jnp.bfloat16)
    folded = folded.reshape(2, fields * 2 * lat_rows, lon_count // 2)
    table = jnp.asarray(half_table(lon_count, np.arange(MM // 2)))
    fourier = jnp.einsum(
        "eril,eal->iera", table, folded, preferred_element_type=jnp.float32
    ).astype(jnp.bfloat16)
    order = (
        wave_list.reshape(-1)[:, None] == lax.broadcasted_iota(jnp.int32, (1, MM // 2), 1)
    ).astype(jnp.bfloat16)
    sent = jnp.einsum(
        "qi,ix->qx", order, fourier.reshape(MM // 2, -1), preferred_element_type=jnp.float32
    ).astype(jnp.bfloat16)
    got = lax.all_to_all(sent.reshape(devices, own_pairs, -1), AXES, 0, 0, tiled=True)
    bands = legendre.shape[2] // lat_rows
    got = got.reshape(bands, devices // bands, own_pairs, 2, 2, fields, 2, lat_rows)
    data = got.transpose(2, 6, 1, 5, 4, 3, 0, 7).reshape(own_pairs, 2, -1, bands * lat_rows)
    products = jnp.einsum("qpxj,qpjc->qpxc", data, legendre, preferred_element_type=jnp.float32)
    products = products.reshape(own_pairs, 2, -1, 2, 2, legendre.shape[3])
    first_wave = own_waves[:, None, None]
    parity = lax.broadcasted_iota(jnp.int32, (1, 2, 1), 1)
    column = lax.broadcasted_iota(jnp.int32, (1, 1, legendre.shape[3]), 2)
    first_count = (MM - first_wave + 1 - parity) // 2
    second_count = (first_wave + 2 - parity) // 2
    in_first = column < first_count
    live = (column < first_count + second_count) & (first_wave < MM)
    use_even = in_first == (first_wave % 2 == 0)
    spectrum = jnp.where(
        live[:, :, None, None],
        jnp.where(use_even[:, :, None, None], products[..., 0, :], products[..., 1, :]),
        0.0,
    )
    return spectrum.astype(jnp.bfloat16)


NT = (((1,), (1,)), ((), ()))
GROUP = 4
HEAD = 1


def repeat_kernel(wave, out):
    out[...] = jnp.broadcast_to(wave[...], out.shape)


def repeated(slot_wave, count):
    whole = pl.BlockSpec(memory_space=pltpu.VMEM)
    return pl.pallas_call(
        repeat_kernel,
        in_specs=[whole],
        out_specs=whole,
        out_shape=jax.ShapeDtypeStruct((count, 1, slot_wave.shape[0]), jnp.int32),
        name="repeated",
    )(slot_wave.reshape(1, 1, -1))


def quarter_order(row):
    low = 4 * ((row % (MM // 4)) // 2)
    return low + (row // (MM // 4)) + (row % 2) * (3 - 2 * (row // (MM // 4)))


def transform_kernel(me, grid, table, out, grid_here, table_here, folded, grid_sems, table_sems):
    fields, _, rows, lons = grid_here.shape
    half = lons // 2
    quarter = half // 2
    turn = (me[0] >> 2) & 3
    grid_copies = [
        pltpu.make_async_copy(grid.at[field], grid_here.at[field], grid_sems.at[field])
        for field in range(fields)
    ]
    table_copies = [
        pltpu.make_async_copy(table.at[part], table_here.at[part], table_sems.at[part])
        for part in range(table.shape[0])
    ]
    for copy in grid_copies + table_copies:
        copy.start()

    def fold(kind, field):
        for row in range(0, rows, 16):
            part = pl.ds(row, 16)
            west = [grid_here[field, side, part, :half].astype(jnp.float32) for side in range(2)]
            east = [grid_here[field, side, part, half:].astype(jnp.float32) for side in range(2)]
            north, south = [
                west[side] + east[side] if kind == 0 else west[side] - east[side]
                for side in range(2)
            ]
            for parity in range(2):
                value = north + south if parity == 0 else north - south
                if kind == 0:
                    left, right = value[:, :quarter], value[:, quarter:]
                    value = jnp.concatenate([left + right, left - right], axis=1)
                place = (field * 2 + parity + turn) & 3
                at = pl.multiple_of(place * rows + row, 16)
                folded[kind, pl.ds(at, 16), :] = value.astype(jnp.bfloat16)

    def product(first, second):
        return lax.dot_general(first, second, NT, preferred_element_type=jnp.float32).astype(
            jnp.bfloat16
        )

    for field in range(fields):
        grid_copies[field].wait()
        fold(0, field)
    table_copies[0].wait()
    waves = table.shape[1]
    half_rows = waves // 2
    for which in range(2):
        lanes = slice(which * quarter, (which + 1) * quarter)
        got = product(table_here[0, :, lanes], folded[0, :, lanes])
        for part in range(2):
            out[part, which * half_rows : (which + 1) * half_rows] = got[
                part * half_rows : (part + 1) * half_rows
            ]
    for field in range(fields):
        fold(1, field)
    for part in range(2):
        table_copies[1 + part].wait()
    got = product(table_here[1:].reshape(2 * waves, half), folded[1])
    for part in range(2):
        out[2 + part] = got[part * waves : (part + 1) * waves]


def transform(me, grid_fields, table):
    fields, _, rows, lons = grid_fields.shape
    parts, waves, half = table.shape
    lanes = fields * 2 * rows
    return pl.pallas_call(
        transform_kernel,
        in_specs=[
            pl.BlockSpec(memory_space=pltpu.SMEM),
            pl.BlockSpec(memory_space=pl.ANY),
            pl.BlockSpec(memory_space=pl.ANY),
        ],
        out_specs=pl.BlockSpec(memory_space=pltpu.VMEM),
        scratch_shapes=[
            pltpu.VMEM(grid_fields.shape, jnp.bfloat16),
            pltpu.VMEM(table.shape, jnp.bfloat16),
            pltpu.VMEM((2, lanes, half), jnp.bfloat16),
            pltpu.SemaphoreType.DMA((fields,)),
            pltpu.SemaphoreType.DMA((parts,)),
        ],
        out_shape=jax.ShapeDtypeStruct((4, waves, lanes), jnp.bfloat16),
        compiler_params=pltpu.CompilerParams(vmem_limit_bytes=24 << 20),
        cost_estimate=pl.CostEstimate(
            flops=6 * waves * half * lanes, bytes_accessed=10 << 20, transcendentals=0
        ),
        name="transform",
    )(me, grid_fields, table)


def transform_table(lon_count):
    full = half_table(lon_count, quarter_order(np.arange(MM // 2)))
    short = full[0, :, :, : lon_count // 4].reshape(2, 2, MM // 4, lon_count // 4)
    short = short.transpose(0, 2, 1, 3).reshape(MM // 2, lon_count // 2)
    return np.stack([short, full[1, 0], full[1, 1]])


def order_kernel(waves, fourier, out, square, picks, rows_f32, staged, sems):
    kinds, count, lanes = fourier.shape
    devices, size, _ = out.shape
    pairs = size // kinds
    slots = devices * pairs
    square[...] = jnp.zeros_like(square)
    for device in range(devices):
        square[device : device + 1, : 2 * pairs] = waves[device]
    square[...] = square[...].T
    number = quarter_order(lax.broadcasted_iota(jnp.int32, (pairs, count), 1))
    firsts = square[pl.ds(0, pairs, stride=2), :]
    for device in range(devices):
        wave = firsts[:, device : device + 1]
        picks[device * pairs : (device + 1) * pairs, :] = (
            jnp.where(wave == number, 1.0, 0.0).astype(jnp.bfloat16)
        )
    for kind in range(kinds):
        got = jnp.dot(picks[...], fourier[kind], preferred_element_type=jnp.float32)
        for tile in range(lanes // 128):
            rows_f32[tile, pl.ds(kind, slots, stride=kinds), :] = got[:, tile * 128 : tile * 128 + 128]
    copies = []
    for device in range(devices):
        for tile in range(lanes // 128):
            staged[device, :, tile * 128 : tile * 128 + 128] = rows_f32[
                tile, device * size : (device + 1) * size, :
            ].astype(jnp.bfloat16)
        if device % 8 == 7:
            part = pl.ds(device - 7, 8)
            copy = pltpu.make_async_copy(staged.at[part], out.at[part], sems.at[device // 8])
            copy.start()
            copies.append(copy)
    for copy in copies:
        copy.wait()


def ordered(waves, fourier, pairs):
    kinds, count, lanes = fourier.shape
    devices = waves.shape[0]
    slots = devices * pairs
    whole = pl.BlockSpec(memory_space=pltpu.VMEM)
    return pl.pallas_call(
        order_kernel,
        in_specs=[whole, whole],
        out_specs=pl.BlockSpec(memory_space=pl.ANY),
        scratch_shapes=[
            pltpu.VMEM((128, 128), jnp.int32),
            pltpu.VMEM((slots, count), jnp.bfloat16),
            pltpu.VMEM((lanes // 128, kinds * slots, 128), jnp.float32),
            pltpu.VMEM((devices, kinds * pairs, lanes), jnp.bfloat16),
            pltpu.SemaphoreType.DMA((devices // 8,)),
        ],
        out_shape=jax.ShapeDtypeStruct((devices, kinds * pairs, lanes), jnp.bfloat16),
        compiler_params=pltpu.CompilerParams(vmem_limit_bytes=24 << 20),
        cost_estimate=pl.CostEstimate(
            flops=2 * slots * kinds * count * lanes, bytes_accessed=4 << 20, transcendentals=0
        ),
        name="ordered",
    )(waves, fourier)


def turned_kernel(table, head, out, last):
    columns, _, lat = table.shape[1:]
    main = columns - 1
    step = pl.program_id(0)
    value = table[0, :main].reshape(2 * main, lat).T

    @pl.when(step < HEAD)
    def _():
        head[jnp.minimum(step, HEAD - 1)] = value

    @pl.when(step >= HEAD)
    def _():
        out[0] = value

    last[0] = table[0, main]


def turned(table):
    pairs, columns, _, lat = table.shape
    wide = 2 * columns - 2
    return pl.pallas_call(
        turned_kernel,
        grid=(pairs,),
        in_specs=[pl.BlockSpec((1, columns, 2, lat), lambda i: (i, 0, 0, 0))],
        out_specs=[
            pl.BlockSpec((HEAD, lat, wide), lambda i: (0, 0, 0)),
            pl.BlockSpec((1, lat, wide), lambda i: (jnp.maximum(i - HEAD, 0), 0, 0)),
            pl.BlockSpec((1, 2, lat), lambda i: (i, 0, 0)),
        ],
        out_shape=[
            jax.ShapeDtypeStruct((HEAD, lat, wide), jnp.bfloat16),
            jax.ShapeDtypeStruct((pairs - HEAD, lat, wide), jnp.bfloat16),
            jax.ShapeDtypeStruct((pairs, 2, lat), jnp.bfloat16),
        ],
        compiler_params=pltpu.CompilerParams(vmem_limit_bytes=24 << 20),
        cost_estimate=pl.CostEstimate(
            flops=20 << 30, bytes_accessed=60 << 20, transcendentals=0
        ),
        name="turned",
    )(table)


def legendre_kernel(waves, blocks, head, table, last, spread, out, held, data, lines, staged, sems, out_sems):
    lat, wide = table.shape[1:]
    pairs = last.shape[0]
    lanes = blocks.shape[2]
    rows = lanes // 4
    columns = wide // 2 + 1
    copies = [
        pltpu.make_async_copy(table.at[pair], held.at[pair], sems.at[pair])
        for pair in range(pairs - HEAD)
    ]
    for copy in copies:
        copy.start()
    lane = lax.broadcasted_iota(jnp.int32, (4 * GROUP, lanes), 1)
    for group in range(pairs // GROUP):
        for half in range(2):
            for field in range(4):
                have = [
                    blocks[
                        (half * 4 + band) * 4 + field, group * 4 * GROUP : (group + 1) * 4 * GROUP, :
                    ].astype(jnp.float32)
                    for band in range(4)
                ]
                for turn in range(4):
                    value = have[-turn % 4]
                    for place in range(1, 4):
                        value = jnp.where(lane >= place * rows, have[(place - turn) % 4], value)
                    if turn:
                        value = pltpu.roll(value, lanes - turn * rows, 1)
                    line = (field * 2 + turn // 2) * 2
                    for pair in range(GROUP):
                        for kind in range(2):
                            data[
                                group * GROUP + pair,
                                turn % 2,
                                pl.ds(kind * 16 + line, 2),
                                half * lanes : (half + 1) * lanes,
                            ] = value[pair * 4 + kind * 2 : pair * 4 + kind * 2 + 2]

    for pair in range(pairs):
        wave = waves[pair]
        for side in range(2):
            value = jnp.sum(
                data[pair, side] * last[pair, side : side + 1].astype(jnp.float32), axis=1, keepdims=True
            )
            first_count = (MM - wave + 1 - side) >> 1
            second_count = (wave + 2 - side) >> 1
            live = (columns - 1 < first_count + second_count) & (wave < MM)
            in_first = jnp.where(columns - 1 < first_count, 1, 0)
            value = jnp.where(in_first != (wave & 1), value[:16], value[16:])
            value = jnp.where(live, value, 0.0).astype(jnp.bfloat16)
            staged[pair, side, :, :, columns - 1 :] = value.reshape(8, 2, 1)

    index = lax.broadcasted_iota(jnp.int32, (32, wide), 1)
    even = index & 1 == 0
    index = index[:16]
    parity, column = index & 1, index >> 1
    written = []
    groups = [GROUP] * (pairs // GROUP - 1) + [GROUP // 2, GROUP // 4, GROUP // 4]
    for group, count in enumerate(groups):
        start = sum(groups[:group])
        for pair in range(start, start + count):
            if pair >= HEAD:
                copies[pair - HEAD].wait()
            matrix = head[pair] if pair < HEAD else held[pair - HEAD]
            here = data[pair].reshape(64, lat).astype(jnp.bfloat16)
            both = jnp.dot(here, matrix, preferred_element_type=jnp.float32)
            value = jnp.where(even, both[:32], both[32:])
            wave = waves[pair]
            first_count = (MM - wave + 1 - parity) >> 1
            second_count = (wave + 2 - parity) >> 1
            live = (column < first_count + second_count) & (wave < MM)
            in_first = jnp.where(column < first_count, 1, 0)
            value = jnp.where(in_first != (wave & 1), value[:16], value[16:])
            lines[pair * 16 : pair * 16 + 16, :] = jnp.where(live, value, 0.0).astype(jnp.bfloat16)

        top = start * 16
        for block in range(wide // 256):
            apart = jnp.dot(
                lines[top : top + count * 16, block * 256 : block * 256 + 256],
                spread[...],
                preferred_element_type=jnp.float32,
            ).astype(jnp.bfloat16)
            for pair in range(count):
                for side in range(2):
                    piece = apart[pair * 16 : pair * 16 + 16, side * 128 : side * 128 + 128]
                    staged[start + pair, side, :, :, block * 128 : block * 128 + 128] = (
                        piece.reshape(8, 2, 128)
                    )
        part = pl.ds(start, count)
        written.append(pltpu.make_async_copy(staged.at[part], out.at[part], out_sems.at[group]))
        written[-1].start()
    for copy in written:
        copy.wait()


def legendre_product(waves, blocks, head, table, last):
    lat, wide = table.shape[1:]
    pairs = last.shape[0]
    columns = wide // 2 + 1
    lane = np.arange(256)
    spread = np.zeros((256, 256), np.float32)
    spread[lane, (lane % 2) * 128 + lane // 2] = 1.0
    whole = pl.BlockSpec(memory_space=pltpu.VMEM)
    return pl.pallas_call(
        legendre_kernel,
        in_specs=[
            pl.BlockSpec(memory_space=pltpu.SMEM),
            whole,
            whole,
            pl.BlockSpec(memory_space=pl.ANY),
            whole,
            whole,
        ],
        out_specs=pl.BlockSpec(memory_space=pl.ANY),
        scratch_shapes=[
            pltpu.VMEM(table.shape, jnp.bfloat16),
            pltpu.VMEM((pairs, 2, 32, lat), jnp.float32),
            pltpu.VMEM((16 * pairs, wide), jnp.bfloat16),
            pltpu.VMEM((pairs, 2, 8, 2, columns), jnp.bfloat16),
            pltpu.SemaphoreType.DMA((pairs - HEAD,)),
            pltpu.SemaphoreType.DMA((pairs // GROUP + 2,)),
        ],
        out_shape=jax.ShapeDtypeStruct((pairs, 2, 8, 2, columns), jnp.bfloat16),
        compiler_params=pltpu.CompilerParams(vmem_limit_bytes=48 << 20),
        cost_estimate=pl.CostEstimate(flops=8 << 30, bytes_accessed=30 << 20, transcendentals=0),
        name="legendre_product",
    )(waves, blocks, head, table, last, jnp.asarray(spread.astype(jnp.bfloat16)))


def local(grid_fields, legendre, slot_wave, *, devices):
    lon_count = grid_fields.shape[3]
    own_pairs = legendre.shape[0]
    me = lax.axis_index(AXES).astype(jnp.int32).reshape(1)
    own_waves = slot_wave.reshape(own_pairs, 2)[:, 0]
    waves = lax.all_to_all(repeated(slot_wave, devices), AXES, 0, 0, tiled=True)
    table = jnp.asarray(transform_table(lon_count))
    fourier = transform(me, HBM(grid_fields), HBM(table))
    sent = ordered(waves, fourier, own_pairs)
    got = lax.all_to_all(sent, AXES, 0, 0, tiled=True)
    head, rows, last = turned(HBM(legendre.transpose(0, 3, 1, 2)))
    return legendre_product(own_waves, got, head, HBM(rows), last)


def HBM(array):
    return pltpu.with_memory_space_constraint(array, pltpu.HBM)


def fits(mesh, grid_fields, legendre):
    fields, _, rows, _ = grid_fields.shape
    return (
        mesh.shape["band"] == 8
        and mesh.shape["fld"] == 4
        and fields == 8
        and rows % 128 == 0
        and rows * 4 // 8 % 128 == 0
        and legendre.shape[3] % 128 == 1
        and legendre.shape[0] == MM // 2
    )


def solution(mesh):
    def run(grid_fields, legendre, slot_wave):
        part = local if fits(mesh, grid_fields, legendre) else general
        return jax.shard_map(
            functools.partial(part, devices=mesh.size),
            mesh=mesh,
            in_specs=(P("fld", None, "band", None), P(AXES, None, None, None), P(AXES)),
            out_specs=P(AXES, None, None, None, None),
            check_vma=False,
        )(grid_fields, legendre, slot_wave)

    return run
```

```python
import functools
import math

import jax
import jax.numpy as jnp
import numpy as np
from jax import lax
from jax.experimental import pallas as pl
from jax.experimental.pallas import tpu as pltpu
from jax.sharding import PartitionSpec as P

MM = 1024
AXES = ("band", "fld")


def half_table(lon_count, index):
    even = np.where(index % 2 == 0, index, MM - 1 - index)
    waves = np.stack([even, MM - 1 - even])
    phase = waves[:, :, None] * np.arange(lon_count // 2)[None, None, :] % lon_count
    angle = phase.astype(np.float32) * np.float32(2.0 * math.pi / lon_count)
    scale = 1.0 / math.sqrt(lon_count)
    angle = angle.astype(np.float64)
    table = np.stack([np.cos(angle) * scale, -np.sin(angle) * scale], axis=1)
    return table.astype(np.float32).astype(jnp.bfloat16)


def general(grid_fields, legendre, slot_wave, *, devices):
    fields, _, lat_rows, lon_count = grid_fields.shape
    own_pairs = legendre.shape[0]
    own_waves = slot_wave.reshape(own_pairs, 2)[:, 0]
    wave_list = lax.all_to_all(
        jnp.broadcast_to(own_waves[None], (devices, own_pairs)), AXES, 0, 0, tiled=True
    )
    west = grid_fields[..., : lon_count // 2].astype(jnp.float32)
    east = grid_fields[..., lon_count // 2 :].astype(jnp.float32)
    halves = jnp.stack([west + east, west - east])
    north = halves[:, :, 0]
    south = halves[:, :, 1]
    folded = jnp.stack([north + south, north - south], axis=2).astype(jnp.bfloat16)
    folded = folded.reshape(2, fields * 2 * lat_rows, lon_count // 2)
    table = jnp.asarray(half_table(lon_count, np.arange(MM // 2)))
    fourier = jnp.einsum(
        "eril,eal->iera", table, folded, preferred_element_type=jnp.float32
    ).astype(jnp.bfloat16)
    order = (
        wave_list.reshape(-1)[:, None] == lax.broadcasted_iota(jnp.int32, (1, MM // 2), 1)
    ).astype(jnp.bfloat16)
    sent = jnp.einsum(
        "qi,ix->qx", order, fourier.reshape(MM // 2, -1), preferred_element_type=jnp.float32
    ).astype(jnp.bfloat16)
    got = lax.all_to_all(sent.reshape(devices, own_pairs, -1), AXES, 0, 0, tiled=True)
    bands = legendre.shape[2] // lat_rows
    got = got.reshape(bands, devices // bands, own_pairs, 2, 2, fields, 2, lat_rows)
    data = got.transpose(2, 6, 1, 5, 4, 3, 0, 7).reshape(own_pairs, 2, -1, bands * lat_rows)
    products = jnp.einsum("qpxj,qpjc->qpxc", data, legendre, preferred_element_type=jnp.float32)
    products = products.reshape(own_pairs, 2, -1, 2, 2, legendre.shape[3])
    first_wave = own_waves[:, None, None]
    parity = lax.broadcasted_iota(jnp.int32, (1, 2, 1), 1)
    column = lax.broadcasted_iota(jnp.int32, (1, 1, legendre.shape[3]), 2)
    first_count = (MM - first_wave + 1 - parity) // 2
    second_count = (first_wave + 2 - parity) // 2
    in_first = column < first_count
    live = (column < first_count + second_count) & (first_wave < MM)
    use_even = in_first == (first_wave % 2 == 0)
    spectrum = jnp.where(
        live[:, :, None, None],
        jnp.where(use_even[:, :, None, None], products[..., 0, :], products[..., 1, :]),
        0.0,
    )
    return spectrum.astype(jnp.bfloat16)


NT = (((1,), (1,)), ((), ()))
GROUP = 4
HEAD = 1


def repeat_kernel(wave, out):
    out[...] = jnp.broadcast_to(wave[...], out.shape)


def repeated(slot_wave, count):
    whole = pl.BlockSpec(memory_space=pltpu.VMEM)
    return pl.pallas_call(
        repeat_kernel,
        in_specs=[whole],
        out_specs=whole,
        out_shape=jax.ShapeDtypeStruct((count, 1, slot_wave.shape[0]), jnp.int32),
        name="repeated",
    )(slot_wave.reshape(1, 1, -1))


def quarter_order(row):
    low = 4 * ((row % (MM // 4)) // 2)
    return low + (row // (MM // 4)) + (row % 2) * (3 - 2 * (row // (MM // 4)))


def transform_kernel(me, grid, table, out, grid_here, table_here, folded, grid_sems, table_sems):
    fields, _, rows, lons = grid_here.shape
    half = lons // 2
    quarter = half // 2
    turn = (me[0] >> 2) & 3
    grid_copies = [
        pltpu.make_async_copy(grid.at[field], grid_here.at[field], grid_sems.at[field])
        for field in range(fields)
    ]
    table_copies = [
        pltpu.make_async_copy(table.at[part], table_here.at[part], table_sems.at[part])
        for part in range(table.shape[0])
    ]
    for copy in grid_copies + table_copies:
        copy.start()

    def fold(kind, field):
        for row in range(0, rows, 16):
            part = pl.ds(row, 16)
            west = [grid_here[field, side, part, :half].astype(jnp.float32) for side in range(2)]
            east = [grid_here[field, side, part, half:].astype(jnp.float32) for side in range(2)]
            north, south = [
                west[side] + east[side] if kind == 0 else west[side] - east[side]
                for side in range(2)
            ]
            for parity in range(2):
                value = north + south if parity == 0 else north - south
                if kind == 0:
                    left, right = value[:, :quarter], value[:, quarter:]
                    value = jnp.concatenate([left + right, left - right], axis=1)
                place = (field * 2 + parity + turn) & 3
                at = pl.multiple_of(place * rows + row, 16)
                folded[kind, pl.ds(at, 16), :] = value.astype(jnp.bfloat16)

    def product(first, second):
        return lax.dot_general(first, second, NT, preferred_element_type=jnp.float32).astype(
            jnp.bfloat16
        )

    for field in range(fields):
        grid_copies[field].wait()
        fold(0, field)
    table_copies[0].wait()
    waves = table.shape[1]
    half_rows = waves // 2
    for which in range(2):
        lanes = slice(which * quarter, (which + 1) * quarter)
        got = product(table_here[0, :, lanes], folded[0, :, lanes])
        for part in range(2):
            out[part, which * half_rows : (which + 1) * half_rows] = got[
                part * half_rows : (part + 1) * half_rows
            ]
    for field in range(fields):
        fold(1, field)
    for part in range(2):
        table_copies[1 + part].wait()
    got = product(table_here[1:].reshape(2 * waves, half), folded[1])
    for part in range(2):
        out[2 + part] = got[part * waves : (part + 1) * waves]


def transform(me, grid_fields, table):
    fields, _, rows, lons = grid_fields.shape
    parts, waves, half = table.shape
    lanes = fields * 2 * rows
    return pl.pallas_call(
        transform_kernel,
        in_specs=[
            pl.BlockSpec(memory_space=pltpu.SMEM),
            pl.BlockSpec(memory_space=pl.ANY),
            pl.BlockSpec(memory_space=pl.ANY),
        ],
        out_specs=pl.BlockSpec(memory_space=pltpu.VMEM),
        scratch_shapes=[
            pltpu.VMEM(grid_fields.shape, jnp.bfloat16),
            pltpu.VMEM(table.shape, jnp.bfloat16),
            pltpu.VMEM((2, lanes, half), jnp.bfloat16),
            pltpu.SemaphoreType.DMA((fields,)),
            pltpu.SemaphoreType.DMA((parts,)),
        ],
        out_shape=jax.ShapeDtypeStruct((4, waves, lanes), jnp.bfloat16),
        compiler_params=pltpu.CompilerParams(vmem_limit_bytes=24 << 20),
        cost_estimate=pl.CostEstimate(
            flops=6 * waves * half * lanes, bytes_accessed=10 << 20, transcendentals=0
        ),
        name="transform",
    )(me, grid_fields, table)


def transform_table(lon_count):
    full = half_table(lon_count, quarter_order(np.arange(MM // 2)))
    short = full[0, :, :, : lon_count // 4].reshape(2, 2, MM // 4, lon_count // 4)
    short = short.transpose(0, 2, 1, 3).reshape(MM // 2, lon_count // 2)
    return np.stack([short, full[1, 0], full[1, 1]])


def order_kernel(waves, fourier, out, square, picks, rows_f32, staged, sems):
    kinds, count, lanes = fourier.shape
    devices, size, _ = out.shape
    pairs = size // kinds
    slots = devices * pairs
    square[...] = jnp.zeros_like(square)
    for device in range(devices):
        square[device : device + 1, : 2 * pairs] = waves[device]
    square[...] = square[...].T
    number = quarter_order(lax.broadcasted_iota(jnp.int32, (pairs, count), 1))
    firsts = square[pl.ds(0, pairs, stride=2), :]
    for device in range(devices):
        wave = firsts[:, device : device + 1]
        picks[device * pairs : (device + 1) * pairs, :] = (
            jnp.where(wave == number, 1.0, 0.0).astype(jnp.bfloat16)
        )
    copies = []
    share = 8
    for first in range(0, devices, share):
        for kind in range(kinds):
            got = jnp.dot(
                picks[first * pairs : (first + share) * pairs, :],
                fourier[kind],
                preferred_element_type=jnp.float32,
            )
            for tile in range(lanes // 128):
                rows_f32[tile, pl.ds(first * size + kind, share * pairs, stride=kinds), :] = got[
                    :, tile * 128 : tile * 128 + 128
                ]
        for device in range(first, first + share):
            for tile in range(lanes // 128):
                staged[device, :, tile * 128 : tile * 128 + 128] = rows_f32[
                    tile, device * size : (device + 1) * size, :
                ].astype(jnp.bfloat16)
        part = pl.ds(first, share)
        copies.append(
            pltpu.make_async_copy(staged.at[part], out.at[part], sems.at[first // share])
        )
        copies[-1].start()
    for copy in copies:
        copy.wait()


def ordered(waves, fourier, pairs):
    kinds, count, lanes = fourier.shape
    devices = waves.shape[0]
    slots = devices * pairs
    whole = pl.BlockSpec(memory_space=pltpu.VMEM)
    return pl.pallas_call(
        order_kernel,
        in_specs=[whole, whole],
        out_specs=pl.BlockSpec(memory_space=pl.ANY),
        scratch_shapes=[
            pltpu.VMEM((128, 128), jnp.int32),
            pltpu.VMEM((slots, count), jnp.bfloat16),
            pltpu.VMEM((lanes // 128, kinds * slots, 128), jnp.float32),
            pltpu.VMEM((devices, kinds * pairs, lanes), jnp.bfloat16),
            pltpu.SemaphoreType.DMA((devices // 8,)),
        ],
        out_shape=jax.ShapeDtypeStruct((devices, kinds * pairs, lanes), jnp.bfloat16),
        compiler_params=pltpu.CompilerParams(vmem_limit_bytes=24 << 20),
        cost_estimate=pl.CostEstimate(
            flops=2 * slots * kinds * count * lanes, bytes_accessed=4 << 20, transcendentals=0
        ),
        name="ordered",
    )(waves, fourier)


def turned_kernel(table, head, out, last):
    columns, _, lat = table.shape[1:]
    main = columns - 1
    step = pl.program_id(0)
    value = table[0, :main].reshape(2 * main, lat).T

    @pl.when(step < HEAD)
    def _():
        head[jnp.minimum(step, HEAD - 1)] = value

    @pl.when(step >= HEAD)
    def _():
        out[0] = value

    last[0] = table[0, main]


def turned(table):
    pairs, columns, _, lat = table.shape
    wide = 2 * columns - 2
    return pl.pallas_call(
        turned_kernel,
        grid=(pairs,),
        in_specs=[pl.BlockSpec((1, columns, 2, lat), lambda i: (i, 0, 0, 0))],
        out_specs=[
            pl.BlockSpec((HEAD, lat, wide), lambda i: (0, 0, 0)),
            pl.BlockSpec((1, lat, wide), lambda i: (jnp.maximum(i - HEAD, 0), 0, 0)),
            pl.BlockSpec((1, 2, lat), lambda i: (i, 0, 0)),
        ],
        out_shape=[
            jax.ShapeDtypeStruct((HEAD, lat, wide), jnp.bfloat16),
            jax.ShapeDtypeStruct((pairs - HEAD, lat, wide), jnp.bfloat16),
            jax.ShapeDtypeStruct((pairs, 2, lat), jnp.bfloat16),
        ],
        compiler_params=pltpu.CompilerParams(vmem_limit_bytes=24 << 20),
        cost_estimate=pl.CostEstimate(
            flops=20 << 30, bytes_accessed=60 << 20, transcendentals=0
        ),
        name="turned",
    )(table)


def legendre_kernel(
    waves, blocks, head, table, last_far, spread_far, out,
    held, data, lines, staged, last, spread, sems, out_sems, side_sems,
):
    lat, wide = table.shape[1:]
    pairs = last.shape[0]
    lanes = blocks.shape[2]
    rows = lanes // 4
    columns = wide // 2 + 1
    copies = [
        pltpu.make_async_copy(table.at[pair], held.at[pair], sems.at[pair])
        for pair in range(pairs - HEAD)
    ]
    for copy in copies[:1]:
        copy.start()
    sides = [
        pltpu.make_async_copy(last_far, last, side_sems.at[0]),
        pltpu.make_async_copy(spread_far, spread, side_sems.at[1]),
    ]
    for copy in sides + copies[1:]:
        copy.start()
    lane = lax.broadcasted_iota(jnp.int32, (4 * GROUP, lanes), 1)

    def prepare(group):
        for half in range(2):
            for field in range(4):
                have = [
                    blocks[
                        (half * 4 + band) * 4 + field, group * 4 * GROUP : (group + 1) * 4 * GROUP, :
                    ].astype(jnp.float32)
                    for band in range(4)
                ]
                for turn in range(4):
                    value = have[-turn % 4]
                    for place in range(1, 4):
                        value = jnp.where(lane >= place * rows, have[(place - turn) % 4], value)
                    if turn:
                        value = pltpu.roll(value, lanes - turn * rows, 1)
                    line = (field * 2 + turn // 2) * 2
                    for pair in range(GROUP):
                        for kind in range(2):
                            data[
                                group * GROUP + pair,
                                turn % 2,
                                pl.ds(kind * 16 + line, 2),
                                half * lanes : (half + 1) * lanes,
                            ] = value[pair * 4 + kind * 2 : pair * 4 + kind * 2 + 2]

    for copy in sides:
        copy.wait()

    def edge(pair):
        wave = waves[pair]
        for side in range(2):
            value = jnp.sum(
                data[pair, side] * last[pair, side : side + 1].astype(jnp.float32), axis=1, keepdims=True
            )
            first_count = (MM - wave + 1 - side) >> 1
            second_count = (wave + 2 - side) >> 1
            live = (columns - 1 < first_count + second_count) & (wave < MM)
            in_first = jnp.where(columns - 1 < first_count, 1, 0)
            value = jnp.where(in_first != (wave & 1), value[:16], value[16:])
            value = jnp.where(live, value, 0.0).astype(jnp.bfloat16)
            staged[pair, side, :, :, columns - 1 :] = value.reshape(8, 2, 1)

    index = lax.broadcasted_iota(jnp.int32, (32, wide), 1)
    even = index & 1 == 0
    index = index[:16]
    parity, column = index & 1, index >> 1
    written = []
    for group in range(pairs // GROUP):
        start, count = group * GROUP, GROUP
        prepare(group)
        for pair in range(start, start + count):
            edge(pair)
        for pair in range(start, start + count):
            if pair >= HEAD:
                copies[pair - HEAD].wait()
            matrix = head[pair] if pair < HEAD else held[pair - HEAD]
            here = data[pair].reshape(64, lat).astype(jnp.bfloat16)
            both = jnp.dot(here, matrix, preferred_element_type=jnp.float32)
            value = jnp.where(even, both[:32], both[32:])
            wave = waves[pair]
            first_count = (MM - wave + 1 - parity) >> 1
            second_count = (wave + 2 - parity) >> 1
            live = (column < first_count + second_count) & (wave < MM)
            in_first = jnp.where(column < first_count, 1, 0)
            value = jnp.where(in_first != (wave & 1), value[:16], value[16:])
            lines[pair * 16 : pair * 16 + 16, :] = jnp.where(live, value, 0.0).astype(jnp.bfloat16)

        top = start * 16
        for block in range(wide // 256):
            apart = jnp.dot(
                lines[top : top + count * 16, block * 256 : block * 256 + 256],
                spread[...],
                preferred_element_type=jnp.float32,
            ).astype(jnp.bfloat16)
            for pair in range(count):
                for side in range(2):
                    piece = apart[pair * 16 : pair * 16 + 16, side * 128 : side * 128 + 128]
                    staged[start + pair, side, :, :, block * 128 : block * 128 + 128] = (
                        piece.reshape(8, 2, 128)
                    )
        part = pl.ds(start, count)
        written.append(pltpu.make_async_copy(staged.at[part], out.at[part], out_sems.at[group]))
        written[-1].start()
    for copy in written:
        copy.wait()


def legendre_product(waves, blocks, head, table, last):
    lat, wide = table.shape[1:]
    pairs = last.shape[0]
    columns = wide // 2 + 1
    lane = np.arange(256)
    spread = np.zeros((256, 256), np.float32)
    spread[lane, (lane % 2) * 128 + lane // 2] = 1.0
    whole = pl.BlockSpec(memory_space=pltpu.VMEM)
    return pl.pallas_call(
        legendre_kernel,
        in_specs=[
            pl.BlockSpec(memory_space=pltpu.SMEM),
            whole,
            whole,
            pl.BlockSpec(memory_space=pl.ANY),
            pl.BlockSpec(memory_space=pl.ANY),
            pl.BlockSpec(memory_space=pl.ANY),
        ],
        out_specs=pl.BlockSpec(memory_space=pl.ANY),
        scratch_shapes=[
            pltpu.VMEM(table.shape, jnp.bfloat16),
            pltpu.VMEM((pairs, 2, 32, lat), jnp.float32),
            pltpu.VMEM((16 * pairs, wide), jnp.bfloat16),
            pltpu.VMEM((pairs, 2, 8, 2, columns), jnp.bfloat16),
            pltpu.VMEM(last.shape, jnp.bfloat16),
            pltpu.VMEM((256, 256), jnp.bfloat16),
            pltpu.SemaphoreType.DMA((pairs - HEAD,)),
            pltpu.SemaphoreType.DMA((pairs // GROUP,)),
            pltpu.SemaphoreType.DMA((2,)),
        ],
        out_shape=jax.ShapeDtypeStruct((pairs, 2, 8, 2, columns), jnp.bfloat16),
        compiler_params=pltpu.CompilerParams(vmem_limit_bytes=48 << 20),
        cost_estimate=pl.CostEstimate(flops=8 << 30, bytes_accessed=30 << 20, transcendentals=0),
        name="legendre_product",
    )(waves, blocks, head, table, last, jnp.asarray(spread.astype(jnp.bfloat16)))


def local(grid_fields, legendre, slot_wave, *, devices):
    lon_count = grid_fields.shape[3]
    own_pairs = legendre.shape[0]
    me = lax.axis_index(AXES).astype(jnp.int32).reshape(1)
    own_waves = slot_wave.reshape(own_pairs, 2)[:, 0]
    waves = lax.all_to_all(repeated(slot_wave, devices), AXES, 0, 0, tiled=True)
    table = jnp.asarray(transform_table(lon_count))
    fourier = transform(me, HBM(grid_fields), HBM(table))
    sent = ordered(waves, fourier, own_pairs)
    got = lax.all_to_all(sent, AXES, 0, 0, tiled=True)
    head, rows, last = turned(HBM(legendre.transpose(0, 3, 1, 2)))
    return legendre_product(own_waves, got, head, HBM(rows), last)


def HBM(array):
    return pltpu.with_memory_space_constraint(array, pltpu.HBM)


def fits(mesh, grid_fields, legendre):
    fields, _, rows, _ = grid_fields.shape
    return (
        mesh.shape["band"] == 8
        and mesh.shape["fld"] == 4
        and fields == 8
        and rows % 128 == 0
        and rows * 4 // 8 % 128 == 0
        and legendre.shape[3] % 128 == 1
        and legendre.shape[0] == MM // 2
    )


def solution(mesh):
    def run(grid_fields, legendre, slot_wave):
        part = local if fits(mesh, grid_fields, legendre) else general
        return jax.shard_map(
            functools.partial(part, devices=mesh.size),
            mesh=mesh,
            in_specs=(P("fld", None, "band", None), P(AXES, None, None, None), P(AXES)),
            out_specs=P(AXES, None, None, None, None),
            check_vma=False,
        )(grid_fields, legendre, slot_wave)

    return run
```

```python
import functools
import math

import jax
import jax.numpy as jnp
import numpy as np
from jax import lax
from jax.experimental import pallas as pl
from jax.experimental.pallas import tpu as pltpu
from jax.sharding import PartitionSpec as P

MM = 1024
AXES = ("band", "fld")


def half_table(lon_count, index):
    even = np.where(index % 2 == 0, index, MM - 1 - index)
    waves = np.stack([even, MM - 1 - even])
    phase = waves[:, :, None] * np.arange(lon_count // 2)[None, None, :] % lon_count
    angle = phase.astype(np.float32) * np.float32(2.0 * math.pi / lon_count)
    scale = 1.0 / math.sqrt(lon_count)
    angle = angle.astype(np.float64)
    table = np.stack([np.cos(angle) * scale, -np.sin(angle) * scale], axis=1)
    return table.astype(np.float32).astype(jnp.bfloat16)


def general(grid_fields, legendre, slot_wave, *, devices):
    fields, _, lat_rows, lon_count = grid_fields.shape
    own_pairs = legendre.shape[0]
    own_waves = slot_wave.reshape(own_pairs, 2)[:, 0]
    wave_list = lax.all_to_all(
        jnp.broadcast_to(own_waves[None], (devices, own_pairs)), AXES, 0, 0, tiled=True
    )
    west = grid_fields[..., : lon_count // 2].astype(jnp.float32)
    east = grid_fields[..., lon_count // 2 :].astype(jnp.float32)
    halves = jnp.stack([west + east, west - east])
    north = halves[:, :, 0]
    south = halves[:, :, 1]
    folded = jnp.stack([north + south, north - south], axis=2).astype(jnp.bfloat16)
    folded = folded.reshape(2, fields * 2 * lat_rows, lon_count // 2)
    table = jnp.asarray(half_table(lon_count, np.arange(MM // 2)))
    fourier = jnp.einsum(
        "eril,eal->iera", table, folded, preferred_element_type=jnp.float32
    ).astype(jnp.bfloat16)
    order = (
        wave_list.reshape(-1)[:, None] == lax.broadcasted_iota(jnp.int32, (1, MM // 2), 1)
    ).astype(jnp.bfloat16)
    sent = jnp.einsum(
        "qi,ix->qx", order, fourier.reshape(MM // 2, -1), preferred_element_type=jnp.float32
    ).astype(jnp.bfloat16)
    got = lax.all_to_all(sent.reshape(devices, own_pairs, -1), AXES, 0, 0, tiled=True)
    bands = legendre.shape[2] // lat_rows
    got = got.reshape(bands, devices // bands, own_pairs, 2, 2, fields, 2, lat_rows)
    data = got.transpose(2, 6, 1, 5, 4, 3, 0, 7).reshape(own_pairs, 2, -1, bands * lat_rows)
    products = jnp.einsum("qpxj,qpjc->qpxc", data, legendre, preferred_element_type=jnp.float32)
    products = products.reshape(own_pairs, 2, -1, 2, 2, legendre.shape[3])
    first_wave = own_waves[:, None, None]
    parity = lax.broadcasted_iota(jnp.int32, (1, 2, 1), 1)
    column = lax.broadcasted_iota(jnp.int32, (1, 1, legendre.shape[3]), 2)
    first_count = (MM - first_wave + 1 - parity) // 2
    second_count = (first_wave + 2 - parity) // 2
    in_first = column < first_count
    live = (column < first_count + second_count) & (first_wave < MM)
    use_even = in_first == (first_wave % 2 == 0)
    spectrum = jnp.where(
        live[:, :, None, None],
        jnp.where(use_even[:, :, None, None], products[..., 0, :], products[..., 1, :]),
        0.0,
    )
    return spectrum.astype(jnp.bfloat16)


NT = (((1,), (1,)), ((), ()))
GROUP = 4
HEAD = 1
PARTS = ((0, 12), (12, 12), (24, 8))


def repeat_kernel(wave, out):
    out[...] = jnp.broadcast_to(wave[...], out.shape)


def repeated(slot_wave, count):
    whole = pl.BlockSpec(memory_space=pltpu.VMEM)
    return pl.pallas_call(
        repeat_kernel,
        in_specs=[whole],
        out_specs=whole,
        out_shape=jax.ShapeDtypeStruct((count, 1, slot_wave.shape[0]), jnp.int32),
        name="repeated",
    )(slot_wave.reshape(1, 1, -1))


def quarter_order(row):
    low = 4 * ((row % (MM // 4)) // 2)
    return low + (row // (MM // 4)) + (row % 2) * (3 - 2 * (row // (MM // 4)))


def transform_kernel(me, grid, table, out, grid_here, table_here, folded, grid_sems, table_sems):
    fields, _, rows, lons = grid_here.shape
    half = lons // 2
    quarter = half // 2
    turn = (me[0] >> 2) & 3
    grid_copies = [
        pltpu.make_async_copy(grid.at[field], grid_here.at[field], grid_sems.at[field])
        for field in range(fields)
    ]
    table_copies = [
        pltpu.make_async_copy(table.at[part], table_here.at[part], table_sems.at[part])
        for part in range(table.shape[0])
    ]
    for copy in grid_copies + table_copies:
        copy.start()

    def fold(kind, field):
        for row in range(0, rows, 16):
            part = pl.ds(row, 16)
            west = [grid_here[field, side, part, :half].astype(jnp.float32) for side in range(2)]
            east = [grid_here[field, side, part, half:].astype(jnp.float32) for side in range(2)]
            north, south = [
                west[side] + east[side] if kind == 0 else west[side] - east[side]
                for side in range(2)
            ]
            for parity in range(2):
                value = north + south if parity == 0 else north - south
                if kind == 0:
                    left, right = value[:, :quarter], value[:, quarter:]
                    value = jnp.concatenate([left + right, left - right], axis=1)
                place = (field * 2 + parity + turn) & 3
                at = pl.multiple_of(place * rows + row, 16)
                folded[kind, pl.ds(at, 16), :] = value.astype(jnp.bfloat16)

    def product(first, second):
        return lax.dot_general(first, second, NT, preferred_element_type=jnp.float32).astype(
            jnp.bfloat16
        )

    for field in range(fields):
        grid_copies[field].wait()
        fold(0, field)
    table_copies[0].wait()
    waves = table.shape[1]
    half_rows = waves // 2
    for which in range(2):
        lanes = slice(which * quarter, (which + 1) * quarter)
        got = product(table_here[0, :, lanes], folded[0, :, lanes])
        for part in range(2):
            out[part, which * half_rows : (which + 1) * half_rows] = got[
                part * half_rows : (part + 1) * half_rows
            ]
    for field in range(fields):
        fold(1, field)
    for part in range(2):
        table_copies[1 + part].wait()
    got = product(table_here[1:].reshape(2 * waves, half), folded[1])
    for part in range(2):
        out[2 + part] = got[part * waves : (part + 1) * waves]


def transform(me, grid_fields, table):
    fields, _, rows, lons = grid_fields.shape
    parts, waves, half = table.shape
    lanes = fields * 2 * rows
    return pl.pallas_call(
        transform_kernel,
        in_specs=[
            pl.BlockSpec(memory_space=pltpu.SMEM),
            pl.BlockSpec(memory_space=pl.ANY),
            pl.BlockSpec(memory_space=pl.ANY),
        ],
        out_specs=pl.BlockSpec(memory_space=pltpu.VMEM),
        scratch_shapes=[
            pltpu.VMEM(grid_fields.shape, jnp.bfloat16),
            pltpu.VMEM(table.shape, jnp.bfloat16),
            pltpu.VMEM((2, lanes, half), jnp.bfloat16),
            pltpu.SemaphoreType.DMA((fields,)),
            pltpu.SemaphoreType.DMA((parts,)),
        ],
        out_shape=jax.ShapeDtypeStruct((4, waves, lanes), jnp.bfloat16),
        compiler_params=pltpu.CompilerParams(vmem_limit_bytes=24 << 20),
        cost_estimate=pl.CostEstimate(
            flops=6 * waves * half * lanes, bytes_accessed=10 << 20, transcendentals=0
        ),
        name="transform",
    )(me, grid_fields, table)


def transform_table(lon_count):
    full = half_table(lon_count, quarter_order(np.arange(MM // 2)))
    short = full[0, :, :, : lon_count // 4].reshape(2, 2, MM // 4, lon_count // 4)
    short = short.transpose(0, 2, 1, 3).reshape(MM // 2, lon_count // 2)
    return np.stack([short, full[1, 0], full[1, 1]])


def order_kernel(waves, fourier, out, square, picks, rows_f32, staged, sems):
    kinds, count, lanes = fourier.shape
    devices, size, _ = out.shape
    pairs = size // kinds
    slots = devices * pairs
    square[...] = jnp.zeros_like(square)
    for device in range(devices):
        square[device : device + 1, : 2 * pairs] = waves[device]
    square[...] = square[...].T
    number = quarter_order(lax.broadcasted_iota(jnp.int32, (pairs, count), 1))
    firsts = square[pl.ds(0, pairs, stride=2), :]
    copies = []
    for part, (first, share) in enumerate(PARTS):
        for device in range(first, first + share):
            picks[device * pairs : (device + 1) * pairs, :] = (
                jnp.where(firsts[:, device : device + 1] == number, 1.0, 0.0).astype(jnp.bfloat16)
            )
        for kind in range(kinds):
            got = jnp.dot(
                picks[first * pairs : (first + share) * pairs, :],
                fourier[kind],
                preferred_element_type=jnp.float32,
            )
            for tile in range(lanes // 128):
                rows_f32[tile, pl.ds(first * size + kind, share * pairs, stride=kinds), :] = got[
                    :, tile * 128 : tile * 128 + 128
                ]
        for device in range(first, first + share):
            for tile in range(lanes // 128):
                staged[device, :, tile * 128 : tile * 128 + 128] = rows_f32[
                    tile, device * size : (device + 1) * size, :
                ].astype(jnp.bfloat16)
        rows = pl.ds(first, share)
        copies.append(pltpu.make_async_copy(staged.at[rows], out.at[rows], sems.at[part]))
        copies[-1].start()
    for copy in copies:
        copy.wait()


def ordered(waves, fourier, pairs):
    kinds, count, lanes = fourier.shape
    devices = waves.shape[0]
    slots = devices * pairs
    whole = pl.BlockSpec(memory_space=pltpu.VMEM)
    return pl.pallas_call(
        order_kernel,
        in_specs=[whole, whole],
        out_specs=pl.BlockSpec(memory_space=pl.ANY),
        scratch_shapes=[
            pltpu.VMEM((128, 128), jnp.int32),
            pltpu.VMEM((slots, count), jnp.bfloat16),
            pltpu.VMEM((lanes // 128, kinds * slots, 128), jnp.float32),
            pltpu.VMEM((devices, kinds * pairs, lanes), jnp.bfloat16),
            pltpu.SemaphoreType.DMA((len(PARTS),)),
        ],
        out_shape=jax.ShapeDtypeStruct((devices, kinds * pairs, lanes), jnp.bfloat16),
        compiler_params=pltpu.CompilerParams(vmem_limit_bytes=24 << 20),
        cost_estimate=pl.CostEstimate(
            flops=2 * slots * kinds * count * lanes, bytes_accessed=4 << 20, transcendentals=0
        ),
        name="ordered",
    )(waves, fourier)


def turned_kernel(table, head, out, last):
    columns, _, lat = table.shape[1:]
    main = columns - 1
    step = pl.program_id(0)
    value = table[0, :main].reshape(2 * main, lat).T

    @pl.when(step < HEAD)
    def _():
        head[jnp.minimum(step, HEAD - 1)] = value

    @pl.when(step >= HEAD)
    def _():
        out[0] = value

    last[0] = table[0, main]


def turned(table):
    pairs, columns, _, lat = table.shape
    wide = 2 * columns - 2
    return pl.pallas_call(
        turned_kernel,
        grid=(pairs,),
        in_specs=[pl.BlockSpec((1, columns, 2, lat), lambda i: (i, 0, 0, 0))],
        out_specs=[
            pl.BlockSpec((HEAD, lat, wide), lambda i: (0, 0, 0)),
            pl.BlockSpec((1, lat, wide), lambda i: (jnp.maximum(i - HEAD, 0), 0, 0)),
            pl.BlockSpec((1, 2, lat), lambda i: (i, 0, 0)),
        ],
        out_shape=[
            jax.ShapeDtypeStruct((HEAD, lat, wide), jnp.bfloat16),
            jax.ShapeDtypeStruct((pairs - HEAD, lat, wide), jnp.bfloat16),
            jax.ShapeDtypeStruct((pairs, 2, lat), jnp.bfloat16),
        ],
        compiler_params=pltpu.CompilerParams(vmem_limit_bytes=24 << 20),
        cost_estimate=pl.CostEstimate(
            flops=20 << 30, bytes_accessed=60 << 20, transcendentals=0
        ),
        name="turned",
    )(table)


def legendre_kernel(
    waves, blocks, head, table, last_far, spread_far, out,
    held, data, lines, staged, last, spread, sems, out_sems, side_sems,
):
    lat, wide = table.shape[1:]
    pairs = last.shape[0]
    lanes = blocks.shape[2]
    rows = lanes // 4
    columns = wide // 2 + 1
    copies = [
        pltpu.make_async_copy(table.at[pair], held.at[pair], sems.at[pair])
        for pair in range(pairs - HEAD)
    ]
    for copy in copies[:1]:
        copy.start()
    sides = [
        pltpu.make_async_copy(last_far, last, side_sems.at[0]),
        pltpu.make_async_copy(spread_far, spread, side_sems.at[1]),
    ]
    for copy in sides + copies[1:]:
        copy.start()
    lane = lax.broadcasted_iota(jnp.int32, (4 * GROUP, lanes), 1)

    def prepare(group):
        for half in range(2):
            for field in range(4):
                have = [
                    blocks[
                        (half * 4 + band) * 4 + field, group * 4 * GROUP : (group + 1) * 4 * GROUP, :
                    ].astype(jnp.float32)
                    for band in range(4)
                ]
                for turn in range(4):
                    value = have[-turn % 4]
                    for place in range(1, 4):
                        value = jnp.where(lane >= place * rows, have[(place - turn) % 4], value)
                    if turn:
                        value = pltpu.roll(value, lanes - turn * rows, 1)
                    line = (field * 2 + turn // 2) * 2
                    for pair in range(GROUP):
                        for kind in range(2):
                            data[
                                group * GROUP + pair,
                                turn % 2,
                                pl.ds(kind * 16 + line, 2),
                                half * lanes : (half + 1) * lanes,
                            ] = value[pair * 4 + kind * 2 : pair * 4 + kind * 2 + 2]

    for copy in sides:
        copy.wait()

    def edge(pair):
        wave = waves[pair]
        for side in range(2):
            value = jnp.sum(
                data[pair, side] * last[pair, side : side + 1].astype(jnp.float32), axis=1, keepdims=True
            )
            first_count = (MM - wave + 1 - side) >> 1
            second_count = (wave + 2 - side) >> 1
            live = (columns - 1 < first_count + second_count) & (wave < MM)
            in_first = jnp.where(columns - 1 < first_count, 1, 0)
            value = jnp.where(in_first != (wave & 1), value[:16], value[16:])
            value = jnp.where(live, value, 0.0).astype(jnp.bfloat16)
            staged[pair, side, :, :, columns - 1 :] = value.reshape(8, 2, 1)

    index = lax.broadcasted_iota(jnp.int32, (32, wide), 1)
    even = index & 1 == 0
    index = index[:16]
    parity, column = index & 1, index >> 1
    written = []
    for group in range(pairs // GROUP):
        start, count = group * GROUP, GROUP
        prepare(group)
        for pair in range(start, start + count):
            edge(pair)
        for pair in range(start, start + count):
            if pair >= HEAD:
                copies[pair - HEAD].wait()
            matrix = head[pair] if pair < HEAD else held[pair - HEAD]
            here = data[pair].reshape(64, lat).astype(jnp.bfloat16)
            both = jnp.dot(here, matrix, preferred_element_type=jnp.float32)
            value = jnp.where(even, both[:32], both[32:])
            wave = waves[pair]
            first_count = (MM - wave + 1 - parity) >> 1
            second_count = (wave + 2 - parity) >> 1
            live = (column < first_count + second_count) & (wave < MM)
            in_first = jnp.where(column < first_count, 1, 0)
            value = jnp.where(in_first != (wave & 1), value[:16], value[16:])
            lines[pair * 16 : pair * 16 + 16, :] = jnp.where(live, value, 0.0).astype(jnp.bfloat16)

        top = start * 16
        for block in range(wide // 256):
            apart = jnp.dot(
                lines[top : top + count * 16, block * 256 : block * 256 + 256],
                spread[...],
                preferred_element_type=jnp.float32,
            ).astype(jnp.bfloat16)
            for pair in range(count):
                for side in range(2):
                    piece = apart[pair * 16 : pair * 16 + 16, side * 128 : side * 128 + 128]
                    staged[start + pair, side, :, :, block * 128 : block * 128 + 128] = (
                        piece.reshape(8, 2, 128)
                    )
        part = pl.ds(start, count)
        written.append(pltpu.make_async_copy(staged.at[part], out.at[part], out_sems.at[group]))
        written[-1].start()
    for copy in written:
        copy.wait()


def legendre_product(waves, blocks, head, table, last):
    lat, wide = table.shape[1:]
    pairs = last.shape[0]
    columns = wide // 2 + 1
    lane = np.arange(256)
    spread = np.zeros((256, 256), np.float32)
    spread[lane, (lane % 2) * 128 + lane // 2] = 1.0
    whole = pl.BlockSpec(memory_space=pltpu.VMEM)
    return pl.pallas_call(
        legendre_kernel,
        in_specs=[
            pl.BlockSpec(memory_space=pltpu.SMEM),
            whole,
            whole,
            pl.BlockSpec(memory_space=pl.ANY),
            pl.BlockSpec(memory_space=pl.ANY),
            pl.BlockSpec(memory_space=pl.ANY),
        ],
        out_specs=pl.BlockSpec(memory_space=pl.ANY),
        scratch_shapes=[
            pltpu.VMEM(table.shape, jnp.bfloat16),
            pltpu.VMEM((pairs, 2, 32, lat), jnp.float32),
            pltpu.VMEM((16 * pairs, wide), jnp.bfloat16),
            pltpu.VMEM((pairs, 2, 8, 2, columns), jnp.bfloat16),
            pltpu.VMEM(last.shape, jnp.bfloat16),
            pltpu.VMEM((256, 256), jnp.bfloat16),
            pltpu.SemaphoreType.DMA((pairs - HEAD,)),
            pltpu.SemaphoreType.DMA((pairs // GROUP,)),
            pltpu.SemaphoreType.DMA((2,)),
        ],
        out_shape=jax.ShapeDtypeStruct((pairs, 2, 8, 2, columns), jnp.bfloat16),
        compiler_params=pltpu.CompilerParams(vmem_limit_bytes=48 << 20),
        cost_estimate=pl.CostEstimate(flops=8 << 30, bytes_accessed=30 << 20, transcendentals=0),
        name="legendre_product",
    )(waves, blocks, head, table, last, jnp.asarray(spread.astype(jnp.bfloat16)))


def local(grid_fields, legendre, slot_wave, *, devices):
    lon_count = grid_fields.shape[3]
    own_pairs = legendre.shape[0]
    me = lax.axis_index(AXES).astype(jnp.int32).reshape(1)
    own_waves = slot_wave.reshape(own_pairs, 2)[:, 0]
    waves = lax.all_to_all(repeated(slot_wave, devices), AXES, 0, 0, tiled=True)
    table = jnp.asarray(transform_table(lon_count))
    fourier = transform(me, HBM(grid_fields), HBM(table))
    sent = ordered(waves, fourier, own_pairs)
    got = lax.all_to_all(sent, AXES, 0, 0, tiled=True)
    head, rows, last = turned(HBM(legendre.transpose(0, 3, 1, 2)))
    return legendre_product(own_waves, got, head, HBM(rows), last)


def HBM(array):
    return pltpu.with_memory_space_constraint(array, pltpu.HBM)


def fits(mesh, grid_fields, legendre):
    fields, _, rows, _ = grid_fields.shape
    return (
        mesh.shape["band"] == 8
        and mesh.shape["fld"] == 4
        and fields == 8
        and rows % 128 == 0
        and rows * 4 // 8 % 128 == 0
        and legendre.shape[3] % 128 == 1
        and legendre.shape[0] == MM // 2
    )


def solution(mesh):
    def run(grid_fields, legendre, slot_wave):
        part = local if fits(mesh, grid_fields, legendre) else general
        return jax.shard_map(
            functools.partial(part, devices=mesh.size),
            mesh=mesh,
            in_specs=(P("fld", None, "band", None), P(AXES, None, None, None), P(AXES)),
            out_specs=P(AXES, None, None, None, None),
            check_vma=False,
        )(grid_fields, legendre, slot_wave)

    return run
```

```python
import functools
import math

import jax
import jax.numpy as jnp
import numpy as np
from jax import lax
from jax.experimental import pallas as pl
from jax.experimental.pallas import tpu as pltpu
from jax.sharding import PartitionSpec as P

MM = 1024
AXES = ("band", "fld")


def half_table(lon_count, index):
    even = np.where(index % 2 == 0, index, MM - 1 - index)
    waves = np.stack([even, MM - 1 - even])
    phase = waves[:, :, None] * np.arange(lon_count // 2)[None, None, :] % lon_count
    angle = phase.astype(np.float32) * np.float32(2.0 * math.pi / lon_count)
    scale = 1.0 / math.sqrt(lon_count)
    angle = angle.astype(np.float64)
    table = np.stack([np.cos(angle) * scale, -np.sin(angle) * scale], axis=1)
    return table.astype(np.float32).astype(jnp.bfloat16)


def general(grid_fields, legendre, slot_wave, *, devices):
    fields, _, lat_rows, lon_count = grid_fields.shape
    own_pairs = legendre.shape[0]
    own_waves = slot_wave.reshape(own_pairs, 2)[:, 0]
    wave_list = lax.all_to_all(
        jnp.broadcast_to(own_waves[None], (devices, own_pairs)), AXES, 0, 0, tiled=True
    )
    west = grid_fields[..., : lon_count // 2].astype(jnp.float32)
    east = grid_fields[..., lon_count // 2 :].astype(jnp.float32)
    halves = jnp.stack([west + east, west - east])
    north = halves[:, :, 0]
    south = halves[:, :, 1]
    folded = jnp.stack([north + south, north - south], axis=2).astype(jnp.bfloat16)
    folded = folded.reshape(2, fields * 2 * lat_rows, lon_count // 2)
    table = jnp.asarray(half_table(lon_count, np.arange(MM // 2)))
    fourier = jnp.einsum(
        "eril,eal->iera", table, folded, preferred_element_type=jnp.float32
    ).astype(jnp.bfloat16)
    order = (
        wave_list.reshape(-1)[:, None] == lax.broadcasted_iota(jnp.int32, (1, MM // 2), 1)
    ).astype(jnp.bfloat16)
    sent = jnp.einsum(
        "qi,ix->qx", order, fourier.reshape(MM // 2, -1), preferred_element_type=jnp.float32
    ).astype(jnp.bfloat16)
    got = lax.all_to_all(sent.reshape(devices, own_pairs, -1), AXES, 0, 0, tiled=True)
    bands = legendre.shape[2] // lat_rows
    got = got.reshape(bands, devices // bands, own_pairs, 2, 2, fields, 2, lat_rows)
    data = got.transpose(2, 6, 1, 5, 4, 3, 0, 7).reshape(own_pairs, 2, -1, bands * lat_rows)
    products = jnp.einsum("qpxj,qpjc->qpxc", data, legendre, preferred_element_type=jnp.float32)
    products = products.reshape(own_pairs, 2, -1, 2, 2, legendre.shape[3])
    first_wave = own_waves[:, None, None]
    parity = lax.broadcasted_iota(jnp.int32, (1, 2, 1), 1)
    column = lax.broadcasted_iota(jnp.int32, (1, 1, legendre.shape[3]), 2)
    first_count = (MM - first_wave + 1 - parity) // 2
    second_count = (first_wave + 2 - parity) // 2
    in_first = column < first_count
    live = (column < first_count + second_count) & (first_wave < MM)
    use_even = in_first == (first_wave % 2 == 0)
    spectrum = jnp.where(
        live[:, :, None, None],
        jnp.where(use_even[:, :, None, None], products[..., 0, :], products[..., 1, :]),
        0.0,
    )
    return spectrum.astype(jnp.bfloat16)


NT = (((1,), (1,)), ((), ()))
GROUP = 4
HEAD = 1
PARTS = ((0, 12), (12, 12), (24, 8))


def repeat_kernel(wave, out):
    out[...] = jnp.broadcast_to(wave[...], out.shape)


def repeated(slot_wave, count):
    whole = pl.BlockSpec(memory_space=pltpu.VMEM)
    return pl.pallas_call(
        repeat_kernel,
        in_specs=[whole],
        out_specs=whole,
        out_shape=jax.ShapeDtypeStruct((count, 1, slot_wave.shape[0]), jnp.int32),
        name="repeated",
    )(slot_wave.reshape(1, 1, -1))


def quarter_order(row):
    low = 4 * ((row % (MM // 4)) // 2)
    return low + (row // (MM // 4)) + (row % 2) * (3 - 2 * (row // (MM // 4)))


def transform_kernel(me, grid, table, out, grid_here, table_here, folded, grid_sems, table_sems):
    fields, _, rows, lons = grid_here.shape
    half = lons // 2
    quarter = half // 2
    turn = (me[0] >> 2) & 3
    grid_copies = [
        pltpu.make_async_copy(grid.at[field], grid_here.at[field], grid_sems.at[field])
        for field in range(fields)
    ]
    table_copies = [
        pltpu.make_async_copy(table.at[part], table_here.at[part], table_sems.at[part])
        for part in range(table.shape[0])
    ]
    for copy in grid_copies + table_copies:
        copy.start()

    def fold(kind, field):
        for row in range(0, rows, 16):
            part = pl.ds(row, 16)
            west = [grid_here[field, side, part, :half].astype(jnp.float32) for side in range(2)]
            east = [grid_here[field, side, part, half:].astype(jnp.float32) for side in range(2)]
            north, south = [
                west[side] + east[side] if kind == 0 else west[side] - east[side]
                for side in range(2)
            ]
            for parity in range(2):
                value = north + south if parity == 0 else north - south
                if kind == 0:
                    left, right = value[:, :quarter], value[:, quarter:]
                    value = jnp.concatenate([left + right, left - right], axis=1)
                place = (field * 2 + parity + turn) & 3
                at = pl.multiple_of(place * rows + row, 16)
                folded[kind, pl.ds(at, 16), :] = value.astype(jnp.bfloat16)

    def product(first, second):
        return lax.dot_general(first, second, NT, preferred_element_type=jnp.float32).astype(
            jnp.bfloat16
        )

    for field in range(fields):
        grid_copies[field].wait()
        fold(0, field)
    table_copies[0].wait()
    waves = table.shape[1]
    half_rows = waves // 2
    for which in range(2):
        lanes = slice(which * quarter, (which + 1) * quarter)
        got = product(table_here[0, :, lanes], folded[0, :, lanes])
        for part in range(2):
            out[part, which * half_rows : (which + 1) * half_rows] = got[
                part * half_rows : (part + 1) * half_rows
            ]
    for field in range(fields):
        fold(1, field)
    for part in range(2):
        table_copies[1 + part].wait()
    got = product(table_here[1:].reshape(2 * waves, half), folded[1])
    for part in range(2):
        out[2 + part] = got[part * waves : (part + 1) * waves]


def transform(me, grid_fields, table):
    fields, _, rows, lons = grid_fields.shape
    parts, waves, half = table.shape
    lanes = fields * 2 * rows
    return pl.pallas_call(
        transform_kernel,
        in_specs=[
            pl.BlockSpec(memory_space=pltpu.SMEM),
            pl.BlockSpec(memory_space=pl.ANY),
            pl.BlockSpec(memory_space=pl.ANY),
        ],
        out_specs=pl.BlockSpec(memory_space=pltpu.VMEM),
        scratch_shapes=[
            pltpu.VMEM(grid_fields.shape, jnp.bfloat16),
            pltpu.VMEM(table.shape, jnp.bfloat16),
            pltpu.VMEM((2, lanes, half), jnp.bfloat16),
            pltpu.SemaphoreType.DMA((fields,)),
            pltpu.SemaphoreType.DMA((parts,)),
        ],
        out_shape=jax.ShapeDtypeStruct((4, waves, lanes), jnp.bfloat16),
        compiler_params=pltpu.CompilerParams(vmem_limit_bytes=24 << 20),
        cost_estimate=pl.CostEstimate(
            flops=6 * waves * half * lanes, bytes_accessed=10 << 20, transcendentals=0
        ),
        name="transform",
    )(me, grid_fields, table)


def transform_table(lon_count):
    full = half_table(lon_count, quarter_order(np.arange(MM // 2)))
    short = full[0, :, :, : lon_count // 4].reshape(2, 2, MM // 4, lon_count // 4)
    short = short.transpose(0, 2, 1, 3).reshape(MM // 2, lon_count // 2)
    return np.stack([short, full[1, 0], full[1, 1]])


def order_kernel(waves, fourier, out, square, picks, rows_f32, staged, sems):
    kinds, count, lanes = fourier.shape
    devices, size, _ = out.shape
    pairs = size // kinds
    slots = devices * pairs
    square[...] = jnp.zeros_like(square)
    for device in range(devices):
        square[device : device + 1, : 2 * pairs] = waves[device]
    square[...] = square[...].T
    number = quarter_order(lax.broadcasted_iota(jnp.int32, (pairs, count), 1))
    firsts = square[pl.ds(0, pairs, stride=2), :]
    copies = []
    for part, (first, share) in enumerate(PARTS):
        for device in range(first, first + share):
            picks[device * pairs : (device + 1) * pairs, :] = (
                jnp.where(firsts[:, device : device + 1] == number, 1.0, 0.0).astype(jnp.bfloat16)
            )
        for kind in range(kinds):
            got = jnp.dot(
                picks[first * pairs : (first + share) * pairs, :],
                fourier[kind],
                preferred_element_type=jnp.float32,
            )
            for tile in range(lanes // 128):
                rows_f32[tile, pl.ds(first * size + kind, share * pairs, stride=kinds), :] = got[
                    :, tile * 128 : tile * 128 + 128
                ]
        for device in range(first, first + share):
            for tile in range(lanes // 128):
                staged[device, :, tile * 128 : tile * 128 + 128] = rows_f32[
                    tile, device * size : (device + 1) * size, :
                ].astype(jnp.bfloat16)
        rows = pl.ds(first, share)
        copies.append(pltpu.make_async_copy(staged.at[rows], out.at[rows], sems.at[part]))
        copies[-1].start()
    for copy in copies:
        copy.wait()


def ordered(waves, fourier, pairs):
    kinds, count, lanes = fourier.shape
    devices = waves.shape[0]
    slots = devices * pairs
    whole = pl.BlockSpec(memory_space=pltpu.VMEM)
    return pl.pallas_call(
        order_kernel,
        in_specs=[whole, whole],
        out_specs=pl.BlockSpec(memory_space=pl.ANY),
        scratch_shapes=[
            pltpu.VMEM((128, 128), jnp.int32),
            pltpu.VMEM((slots, count), jnp.bfloat16),
            pltpu.VMEM((lanes // 128, kinds * slots, 128), jnp.float32),
            pltpu.VMEM((devices, kinds * pairs, lanes), jnp.bfloat16),
            pltpu.SemaphoreType.DMA((len(PARTS),)),
        ],
        out_shape=jax.ShapeDtypeStruct((devices, kinds * pairs, lanes), jnp.bfloat16),
        compiler_params=pltpu.CompilerParams(vmem_limit_bytes=24 << 20),
        cost_estimate=pl.CostEstimate(
            flops=2 * slots * kinds * count * lanes, bytes_accessed=4 << 20, transcendentals=0
        ),
        name="ordered",
    )(waves, fourier)


def turned_kernel(table, head, out, last):
    columns, _, lat = table.shape[1:]
    main = columns - 1
    step = pl.program_id(0)
    value = table[0, :main].reshape(2 * main, lat).T

    @pl.when(step < HEAD)
    def _():
        head[jnp.minimum(step, HEAD - 1)] = value

    @pl.when(step >= HEAD)
    def _():
        out[0] = value

    last[0] = table[0, main]


def turned(table):
    pairs, columns, _, lat = table.shape
    wide = 2 * columns - 2
    return pl.pallas_call(
        turned_kernel,
        grid=(pairs,),
        in_specs=[pl.BlockSpec((1, columns, 2, lat), lambda i: (i, 0, 0, 0))],
        out_specs=[
            pl.BlockSpec((HEAD, lat, wide), lambda i: (0, 0, 0)),
            pl.BlockSpec((1, lat, wide), lambda i: (jnp.maximum(i - HEAD, 0), 0, 0)),
            pl.BlockSpec((1, 2, lat), lambda i: (i, 0, 0)),
        ],
        out_shape=[
            jax.ShapeDtypeStruct((HEAD, lat, wide), jnp.bfloat16),
            jax.ShapeDtypeStruct((pairs - HEAD, lat, wide), jnp.bfloat16),
            jax.ShapeDtypeStruct((pairs, 2, lat), jnp.bfloat16),
        ],
        compiler_params=pltpu.CompilerParams(vmem_limit_bytes=24 << 20),
        cost_estimate=pl.CostEstimate(
            flops=20 << 30, bytes_accessed=60 << 20, transcendentals=0
        ),
        name="turned",
    )(table)


def legendre_kernel(
    waves, blocks, head, table, last_far, spread_far, out,
    held, data, lines, staged, last, spread, sems, out_sems, side_sems,
):
    lat, wide = table.shape[1:]
    pairs = last.shape[0]
    lanes = blocks.shape[2]
    rows = lanes // 4
    columns = wide // 2 + 1
    copies = [
        pltpu.make_async_copy(table.at[pair], held.at[pair], sems.at[pair])
        for pair in range(pairs - HEAD)
    ]
    for copy in copies[:1]:
        copy.start()
    sides = [
        pltpu.make_async_copy(last_far, last, side_sems.at[0]),
        pltpu.make_async_copy(spread_far, spread, side_sems.at[1]),
    ]
    for copy in sides + copies[1:]:
        copy.start()
    lane = lax.broadcasted_iota(jnp.int32, (4 * GROUP, lanes), 1)

    def prepare(group):
        for half in range(2):
            for field in range(4):
                have = [
                    blocks[
                        (half * 4 + band) * 4 + field, group * 4 * GROUP : (group + 1) * 4 * GROUP, :
                    ].astype(jnp.float32)
                    for band in range(4)
                ]
                for turn in range(4):
                    value = have[-turn % 4]
                    for place in range(1, 4):
                        value = jnp.where(lane >= place * rows, have[(place - turn) % 4], value)
                    if turn:
                        value = pltpu.roll(value, lanes - turn * rows, 1)
                    line = (field * 2 + turn // 2) * 2
                    for pair in range(GROUP):
                        for kind in range(2):
                            data[
                                group * GROUP + pair,
                                turn % 2,
                                pl.ds(kind * 16 + line, 2),
                                half * lanes : (half + 1) * lanes,
                            ] = value[pair * 4 + kind * 2 : pair * 4 + kind * 2 + 2]

    for copy in sides:
        copy.wait()

    def edge(pair):
        wave = waves[pair]
        for side in range(2):
            value = jnp.sum(
                data[pair, side] * last[pair, side : side + 1].astype(jnp.float32), axis=1, keepdims=True
            )
            first_count = (MM - wave + 1 - side) >> 1
            second_count = (wave + 2 - side) >> 1
            live = (columns - 1 < first_count + second_count) & (wave < MM)
            in_first = jnp.where(columns - 1 < first_count, 1, 0)
            value = jnp.where(in_first != (wave & 1), value[:16], value[16:])
            value = jnp.where(live, value, 0.0).astype(jnp.bfloat16)
            staged[pair, side, :, :, columns - 1 :] = value.reshape(8, 2, 1)

    index = lax.broadcasted_iota(jnp.int32, (32, wide), 1)
    even = index & 1 == 0
    index = index[:16]
    parity, column = index & 1, index >> 1
    written = []
    for group in range(pairs // GROUP):
        start, count = group * GROUP, GROUP
        if group == 0:
            prepare(0)
        for pair in range(start, start + count):
            edge(pair)
        for pair in range(start, start + count):
            if pair == start + count - 1 and start + count < pairs:
                prepare(group + 1)
            if pair >= HEAD:
                copies[pair - HEAD].wait()
            matrix = head[pair] if pair < HEAD else held[pair - HEAD]
            here = data[pair].reshape(64, lat).astype(jnp.bfloat16)
            both = jnp.dot(here, matrix, preferred_element_type=jnp.float32)
            value = jnp.where(even, both[:32], both[32:])
            wave = waves[pair]
            first_count = (MM - wave + 1 - parity) >> 1
            second_count = (wave + 2 - parity) >> 1
            live = (column < first_count + second_count) & (wave < MM)
            in_first = jnp.where(column < first_count, 1, 0)
            value = jnp.where(in_first != (wave & 1), value[:16], value[16:])
            lines[pair * 16 : pair * 16 + 16, :] = jnp.where(live, value, 0.0).astype(jnp.bfloat16)

        top = start * 16
        for block in range(wide // 256):
            apart = jnp.dot(
                lines[top : top + count * 16, block * 256 : block * 256 + 256],
                spread[...],
                preferred_element_type=jnp.float32,
            ).astype(jnp.bfloat16)
            for pair in range(count):
                for side in range(2):
                    piece = apart[pair * 16 : pair * 16 + 16, side * 128 : side * 128 + 128]
                    staged[start + pair, side, :, :, block * 128 : block * 128 + 128] = (
                        piece.reshape(8, 2, 128)
                    )
        part = pl.ds(start, count)
        written.append(pltpu.make_async_copy(staged.at[part], out.at[part], out_sems.at[group]))
        written[-1].start()
    for copy in written:
        copy.wait()


def legendre_product(waves, blocks, head, table, last):
    lat, wide = table.shape[1:]
    pairs = last.shape[0]
    columns = wide // 2 + 1
    lane = np.arange(256)
    spread = np.zeros((256, 256), np.float32)
    spread[lane, (lane % 2) * 128 + lane // 2] = 1.0
    whole = pl.BlockSpec(memory_space=pltpu.VMEM)
    return pl.pallas_call(
        legendre_kernel,
        in_specs=[
            pl.BlockSpec(memory_space=pltpu.SMEM),
            whole,
            whole,
            pl.BlockSpec(memory_space=pl.ANY),
            pl.BlockSpec(memory_space=pl.ANY),
            pl.BlockSpec(memory_space=pl.ANY),
        ],
        out_specs=pl.BlockSpec(memory_space=pl.ANY),
        scratch_shapes=[
            pltpu.VMEM(table.shape, jnp.bfloat16),
            pltpu.VMEM((pairs, 2, 32, lat), jnp.float32),
            pltpu.VMEM((16 * pairs, wide), jnp.bfloat16),
            pltpu.VMEM((pairs, 2, 8, 2, columns), jnp.bfloat16),
            pltpu.VMEM(last.shape, jnp.bfloat16),
            pltpu.VMEM((256, 256), jnp.bfloat16),
            pltpu.SemaphoreType.DMA((pairs - HEAD,)),
            pltpu.SemaphoreType.DMA((pairs // GROUP,)),
            pltpu.SemaphoreType.DMA((2,)),
        ],
        out_shape=jax.ShapeDtypeStruct((pairs, 2, 8, 2, columns), jnp.bfloat16),
        compiler_params=pltpu.CompilerParams(vmem_limit_bytes=48 << 20),
        cost_estimate=pl.CostEstimate(flops=8 << 30, bytes_accessed=30 << 20, transcendentals=0),
        name="legendre_product",
    )(waves, blocks, head, table, last, jnp.asarray(spread.astype(jnp.bfloat16)))


def local(grid_fields, legendre, slot_wave, *, devices):
    lon_count = grid_fields.shape[3]
    own_pairs = legendre.shape[0]
    me = lax.axis_index(AXES).astype(jnp.int32).reshape(1)
    own_waves = slot_wave.reshape(own_pairs, 2)[:, 0]
    waves = lax.all_to_all(repeated(slot_wave, devices), AXES, 0, 0, tiled=True)
    table = jnp.asarray(transform_table(lon_count))
    fourier = transform(me, HBM(grid_fields), HBM(table))
    sent = ordered(waves, fourier, own_pairs)
    got = lax.all_to_all(sent, AXES, 0, 0, tiled=True)
    head, rows, last = turned(HBM(legendre.transpose(0, 3, 1, 2)))
    return legendre_product(own_waves, got, head, HBM(rows), last)


def HBM(array):
    return pltpu.with_memory_space_constraint(array, pltpu.HBM)


def fits(mesh, grid_fields, legendre):
    fields, _, rows, _ = grid_fields.shape
    return (
        mesh.shape["band"] == 8
        and mesh.shape["fld"] == 4
        and fields == 8
        and rows % 128 == 0
        and rows * 4 // 8 % 128 == 0
        and legendre.shape[3] % 128 == 1
        and legendre.shape[0] == MM // 2
    )


def solution(mesh):
    def run(grid_fields, legendre, slot_wave):
        part = local if fits(mesh, grid_fields, legendre) else general
        return jax.shard_map(
            functools.partial(part, devices=mesh.size),
            mesh=mesh,
            in_specs=(P("fld", None, "band", None), P(AXES, None, None, None), P(AXES)),
            out_specs=P(AXES, None, None, None, None),
            check_vma=False,
        )(grid_fields, legendre, slot_wave)

    return run
```
